256 devices in a mesh: blk: 64 (over z, y, x_lo), rep: 4 (over x_hi, core).
Axes of the slice: x: 4 (x_hi: 2, x_lo: 2; x = x_hi * 2 + x_lo), y: 4, z: 8, core: 2. Of those that a mesh axis runs over, the one named last changes fastest.
Arguments:
- embeddings: bfloat16 [65536, 400], P('blk'), may hold values from -1.5 to 1.5
- relations: bfloat16 [2, 400, 400], replicated, may hold values from -0.3125 to 0.3125
- source_index: int32 [2, 256000], P(None, ('blk', 'rep')), may hold values from 0 to 1023
- target_index: int32 [2, 256000], P(None, ('blk', 'rep')), may hold values from 0 to 1023
- negative_index: int32 [2, 512, 1000], P(None, ('blk', 'rep')), may hold values from 0 to 1023
- span_relation: int32 [2, 512], P(None, ('blk', 'rep')), may hold values from 0 to 1
- edge_count: int32 [2, 256], P(None, ('blk', 'rep')), may hold values from 0 to 1000, as said below
Outputs:
- entity_grad: float32 [65536, 400], P(('blk', 'rep'))
- relation_grad: float32 [2, 400, 400], replicated
The draws below stay inside these ranges and needn't reach their ends.
Inputs may be any that keep to these rules, and one draw needn't show every extreme that they name: For each step and each group of 4 consecutive devices u (those with one blk index), the numbers of spans with a live edge, ceil(edge_count / 500) summed over the group, equal 4; in each such group one device has all 1000 edge slots live.
All inputs are finite; a program needn't handle non-finite values.
Results may differ from the reference program's by a relative error of at most 0.003.
Values may be sent and summed in bfloat16 or wider, within the bound.
A program may use at most 64 MiB of HBM per device.

```python
import jax
import jax.numpy as jnp
from jax import lax

D = 400
NEGS = 1000
SPAN = 500
SLOTS = 2
STEPS = 2
RELS = 2
ENT_DEV = 1024
ENTITIES = 65536
SPANS = 512
EDGES = 256000
N_BLK = 64
N_REP = 4


def draw_edge_count(key, part):
    key = jax.random.fold_in(key, 7)
    spare = N_REP * SLOTS // 2 - SLOTS
    keys = jax.random.split(key, STEPS * N_BLK)

    def group(one_key):
        first, second = jax.random.split(one_key)
        order = jax.random.permutation(first, N_REP)
        placing = jnp.argsort(order).astype(jnp.int32)
        light = jax.random.randint(second, (N_REP,), 1, SPAN + 1)
        return jnp.where(placing == 0, SLOTS * SPAN, jnp.where(placing <= spare, light, 0)).astype(jnp.int32)
    return jax.vmap(group)(keys).reshape(STEPS, N_BLK * N_REP)


def set_ends(entries, rng, low, largest):
    place = [jax.random.randint(jax.random.fold_in(rng, axis), (), 0, length) for axis, length in enumerate(entries.shape)]
    longest = entries.shape.index(max(entries.shape))
    neighbour = place[:longest] + [(place[longest] + 1) % entries.shape[longest]] + place[longest + 1:]
    return entries.at[tuple(place)].set(low).at[tuple(neighbour)].set(largest)


def block_levels(stream_key, dims, pieces, smallest, largest):
    gain, own = 1.0, jax.random.fold_in(stream_key, 6)
    for axis_at, shards_of in pieces:
        draws = jnp.exp(jax.random.uniform(jax.random.fold_in(own, axis_at), (shards_of,), jnp.float32, smallest / len(pieces), largest / len(pieces)))
        gain = gain * jnp.repeat(draws, dims[axis_at] // shards_of).reshape([-1 if axis == axis_at else 1 for axis in range(len(dims))])
    return gain


def bell_draw(rng, extent, spread, limit, shards=(), kind=jnp.bfloat16):
    gain = block_levels(rng, extent, shards, -0.22, 0.18) if shards else 1.0
    array = jax.random.normal(rng, extent, jnp.float32) * spread * gain
    return jnp.minimum(jnp.maximum(array, -limit), limit).astype(kind)


def setup_inputs(seed: int = 0) -> dict:
    splits = jax.random.split(jax.random.key(seed), 8)
    embeddings = bell_draw(splits[0], (ENTITIES, D), 0.22, 1.5, ((0, 64),))
    relations = bell_draw(splits[1], (RELS, D, D), D ** -0.5, 0.3125)
    source_index = set_ends(jax.random.randint(splits[2], (STEPS, EDGES), 0, ENT_DEV), jax.random.fold_in(splits[2], 1), 0, ENT_DEV - 1).astype(jnp.int32)
    target_index = set_ends(jax.random.randint(splits[3], (STEPS, EDGES), 0, ENT_DEV), jax.random.fold_in(splits[3], 1), 0, ENT_DEV - 1).astype(jnp.int32)
    negative_index = set_ends(jax.random.randint(splits[4], (STEPS, SPANS, NEGS), 0, ENT_DEV), jax.random.fold_in(splits[4], 1), 0, ENT_DEV - 1).astype(jnp.int32)
    span_relation = set_ends(jax.random.randint(splits[5], (STEPS, SPANS), 0, RELS), jax.random.fold_in(splits[5], 1), 0, RELS - 1).astype(jnp.int32)
    edge_count = draw_edge_count(jax.random.fold_in(splits[7], 71), 0)
    return dict(embeddings=embeddings, relations=relations, source_index=source_index, target_index=target_index, negative_index=negative_index, span_relation=span_relation, edge_count=edge_count)


def span_grads(source_vectors, target_vectors, negative_vectors, operator, live, neg_scale):
    query = jnp.dot(source_vectors, operator, preferred_element_type=jnp.float32).astype(jnp.bfloat16)
    query_wide = query.astype(jnp.float32)
    positive = jnp.sum(query_wide * target_vectors.astype(jnp.float32), axis=1)
    negative = lax.dot_general(query, negative_vectors, (((1,), (1,)), ((), ())), preferred_element_type=jnp.float32)
    positive_grad = -live * jax.nn.sigmoid(-positive)
    weight = live * neg_scale
    negative_grad = (jax.nn.sigmoid(negative) * weight[:, None]).astype(jnp.bfloat16)
    query_grad = (positive_grad[:, None] * target_vectors.astype(jnp.float32)
                  + jnp.dot(negative_grad, negative_vectors, preferred_element_type=jnp.float32)).astype(jnp.bfloat16)
    source_grad = lax.dot_general(query_grad, operator, (((1,), (1,)), ((), ())), preferred_element_type=jnp.float32)
    target_grad = positive_grad[:, None] * query_wide
    negative_rows_grad = lax.dot_general(negative_grad, query, (((0,), (0,)), ((), ())), preferred_element_type=jnp.float32)
    operator_grad = lax.dot_general(source_vectors, query_grad, (((0,), (0,)), ((), ())), preferred_element_type=jnp.float32)
    return source_grad, target_grad, negative_rows_grad, operator_grad


def reference(embeddings, relations, source_index, target_index, negative_index, span_relation, edge_count):
    neg_scale = NEGS ** -0.5
    entity_sum = jnp.zeros(embeddings.shape, jnp.float32)
    operator_sum = jnp.zeros(relations.shape, jnp.float32)
    span_ids = jnp.arange(SPANS, dtype=jnp.int32)
    for step in range(STEPS):
        def account(carry, span):
            device = span // SLOTS
            slot = span % SLOTS
            block = device // N_REP
            source_base = block * ENT_DEV
            target_base = ((block - step - 1) % N_BLK) * ENT_DEV
            source_rows = lax.dynamic_slice_in_dim(source_index[step], span * SPAN, SPAN) + source_base
            target_rows = lax.dynamic_slice_in_dim(target_index[step], span * SPAN, SPAN) + target_base
            negative_rows = negative_index[step][span] + target_base
            relation_id = span_relation[step][span]
            live_count = jnp.clip(edge_count[step][device] - slot * SPAN, 0, SPAN)

            def compute(state):
                entity_acc, operator_acc = state
                live = (jnp.arange(SPAN, dtype=jnp.int32) < live_count).astype(jnp.float32)
                source_grad, target_grad, negative_rows_grad, operator_grad = span_grads(
                    embeddings[source_rows], embeddings[target_rows], embeddings[negative_rows],
                    relations[relation_id], live, neg_scale)
                entity_acc = entity_acc.at[source_rows].add(source_grad)
                entity_acc = entity_acc.at[target_rows].add(target_grad)
                entity_acc = entity_acc.at[negative_rows].add(negative_rows_grad)
                operator_acc = operator_acc.at[relation_id].add(operator_grad)
                return entity_acc, operator_acc

            def keep(state):
                return state

            return lax.cond(live_count > 0, compute, keep, carry), None

        (entity_sum, operator_sum), unused = lax.scan(account, (entity_sum, operator_sum), span_ids)
    return entity_sum, operator_sum
```

```python
import functools

import jax
import jax.numpy as jnp
from jax import lax
from jax.experimental import pallas as pl
from jax.experimental.pallas import tpu as pltpu
from jax.sharding import PartitionSpec as P

MESH = pl.DeviceIdType.MESH
F32, BF16, I32 = jnp.float32, jnp.bfloat16, jnp.int32
PAD = 512
TILES = 80


def dot(a, b):
    return lax.dot_general(a, b, (((1,), (0,)), ((), ())), preferred_element_type=F32)


def dot_nt(a, b):
    return lax.dot_general(a, b, (((1,), (1,)), ((), ())), preferred_element_type=F32)


def eye(n):
    return (
        lax.broadcasted_iota(I32, (n, n), 0) == lax.broadcasted_iota(I32, (n, n), 1)
    ).astype(F32).astype(BF16)


def onehot(rows, base, index):
    shape = (rows, index.shape[1])
    return (lax.broadcasted_iota(I32, shape, 0) + base == index).astype(F32).astype(BF16)


def kernel(
    n_y, n_z, span, negs,
    emb, rel, src, tgt, neg, srel, ecnt,
    ent_out, rel_out,
    embt, opt, raw, lists, sel, ohs, svt, qt, cnt, slabt, slab, oht, ngm, cm, qhi, qlo, sgt,
    acc, acc_in, red, r1, s1, r2, s2, r3, g3, g2, g1, g_other,
    tsum, tsum_in, ret, ret_in, ssum, ssum_in, half, half_in,
    idx_s, idx_r, slab_s, slab_r, fwd_s, fwd_r, ar0_s, ar0_r, ar1_s, ar1_r, ar2_s, ar2_r, ar3_s, ar3_r,
    ag3_s, ag3_r, ag2_s, ag2_r, ag1_s, ag1_r, ag0_s, ag0_r, tx_s, tx_r, ret_s, ret_r, sx_s, sx_r, sy_s, sy_r,
):
    width = emb.shape[1]
    n_blk = 2 * n_y * n_z
    quarter = emb.shape[0] // 4
    b, r = lax.axis_index("blk"), lax.axis_index("rep")
    xh, core = r // 2, lax.rem(r, 2)
    xl, y, z = lax.rem(b, 2), lax.rem(b // 2, n_y), b // (2 * n_y)
    x = xh * 2 + xl
    sibling = (b, xh * 2 + 1 - core)
    mate = (b, (1 - xh) * 2 + core)

    def along_blk(k):
        return (lax.rem(b + k + n_blk, n_blk), r)

    def along_rep(k):
        return (b, lax.rem(r + k, 4))

    def x_at(k):
        return lax.rem(x + k, 4)

    def y_at(k):
        return lax.rem(y + k, n_y)

    def z_at(k):
        return lax.rem(z + k, n_z)

    def along_x(k):
        there = x_at(k)
        return ((z * n_y + y) * 2 + lax.rem(there, 2), (there // 2) * 2 + core)

    def along_y(k):
        return ((z * n_y + y_at(k)) * 2 + xl, r)

    def along_z(k):
        return ((z_at(k) * n_y + y) * 2 + xl, r)

    def send(source, target, sent, received, device):
        copy = pltpu.make_async_remote_copy(
            src_ref=source, dst_ref=target, send_sem=sent, recv_sem=received,
            device_id=device, device_id_type=MESH,
        )
        copy.start()
        return copy

    barrier = pltpu.get_barrier_semaphore()
    peers = [along_blk(k) for k in (1, 2, -1, -2)] + [along_rep(k) for k in (1, 2, 3)]
    peers += [along_x(k) for k in (1, 2, 3)] + [along_y(k) for k in range(1, n_y)]
    peers += [along_z(k) for k in range(1, n_z)]
    for peer in peers:
        pl.semaphore_signal(barrier, inc=1, device_id=peer, device_id_type=MESH)

    lane = lax.broadcasted_iota(I32, (8, 1024), 1)
    row = lax.broadcasted_iota(I32, (8, 1024), 0)
    raw[...] = jnp.zeros(raw.shape, I32)
    raw[0, 0:2, 0 : 2 * span] = src[...]
    raw[0, 2:4, 0 : 2 * span] = tgt[...]
    for s in range(2):
        raw[1, 2 * s : 2 * s + 2, 0:negs] = neg[s]
    edges = raw[0]
    second = pltpu.roll(edges, PAD - span, 1)
    edges = jnp.where(lane < PAD, edges, second)
    negatives = raw[1]
    packed = jnp.zeros((8, 1024), I32)
    for s in range(2):
        words = edges[s : s + 1] + edges[2 + s : 3 + s] * 65536
        packed = jnp.where(row == 4 * s, words, packed)
        words = negatives[2 * s : 2 * s + 1] + negatives[2 * s + 1 : 2 * s + 2] * 65536
        packed = jnp.where(row == 4 * s + 1, words, packed)
        for k in range(2):
            live = jnp.clip(ecnt[s, 0] - k * span, 0, span)
            packed = jnp.where(row == 4 * s + 2 + k, srel[s, k] + live * 65536, packed)
    lists[r] = packed

    unit = eye(width)
    for q in range(4):
        embt[q] = dot_nt(unit, emb[q * quarter : (q + 1) * quarter, :]).astype(BF16)
    for k in range(2):
        opt[k] = dot_nt(unit, rel[k]).astype(BF16)
    acc[...] = jnp.zeros(acc.shape, F32)
    s1[...] = jnp.zeros(s1.shape, F32)
    s2[...] = jnp.zeros(s2.shape, F32)

    pl.semaphore_wait(barrier, len(peers))

    index_copies = [
        send(lists.at[r], lists.at[r], idx_s.at[k - 1], idx_r.at[k - 1], along_rep(k))
        for k in (1, 2, 3)
    ]
    slab_copies = [
        send(embt.at[r], slabt.at[s, core], slab_s.at[s], slab_r.at[s], along_blk(s + 1))
        for s in range(2)
    ]
    for copy in index_copies:
        copy.wait()

    for s in range(2):
        before = jnp.zeros((1, 1024), I32)
        edge_words = [jnp.zeros((1, PAD), I32) for j in range(2)]
        negative_words = [jnp.zeros((1, 1024), I32) for j in range(2)]
        meta_words = [jnp.zeros((1, 1024), I32) for j in range(2)]
        for d in range(4):
            rows = lists[d]
            for k in range(2):
                meta = rows[4 * s + 2 + k : 4 * s + 3 + k]
                alive = (meta >= 65536).astype(I32)
                both = rows[4 * s + 1 : 4 * s + 2]
                negative = (both & 65535) if k == 0 else (both >> 16)
                edge = rows[4 * s : 4 * s + 1, k * PAD : (k + 1) * PAD]
                for j in range(2):
                    mine = alive * (before == 2 * core + j).astype(I32)
                    edge_words[j] += edge * mine[:, :PAD]
                    negative_words[j] += negative * mine
                    meta_words[j] += meta * mine
                before = before + alive
        lane1 = lax.broadcasted_iota(I32, (1, 1024), 1)
        for j in range(2):
            valid = lane1[:, :PAD] < (meta_words[j][:, :PAD] >> 16)
            at = 2 * s + j
            sel[at, 0:1, 0:PAD] = jnp.where(valid, edge_words[j] & 65535, -1)
            sel[at, 1:2, 0:PAD] = jnp.where(valid, edge_words[j] >> 16, -1)
            sel[at, 2:3, :] = jnp.where(lane1 < negs, negative_words[j], -1)
            sel[at, 3:4, :] = meta_words[j] & 1
            sel[at, 4:5, 0:PAD] = valid.astype(I32)

    def operator(table, at):
        second = sel[at, 3:4, 0:width].astype(F32)
        return (
            table[0].astype(F32) * (1.0 - second) + table[1].astype(F32) * second
        ).astype(BF16)

    def queries(s):
        def body(j, carry):
            at = 2 * s + j
            rows = sel[at, 0:1, 0:PAD]
            total = jnp.zeros((width, PAD), F32)
            for q in range(4):
                picked = onehot(quarter, q * quarter, rows)
                ohs[at, q] = picked
                total += dot(embt[q], picked)
            vectors = total.astype(BF16)
            svt[at] = vectors
            qt[at] = dot(operator(opt, at), vectors).astype(BF16)
            ones = jnp.ones((1024, 128), BF16)
            for h in range(2):
                cnt[at, h] = dot(onehot(quarter, (2 * xh + h) * quarter, sel[at, 2:3, :]), ones)
            return carry

        lax.fori_loop(0, 2, body, 0)

    def forward(s):
        slab_copies[s].wait_recv()
        return send(
            slabt.at[s, core], slabt.at[s, core], fwd_s.at[s], fwd_r.at[s], sibling
        )

    chunk = 128

    def score(s):
        turn = eye(quarter)
        for h in range(2):
            slab[h] = dot_nt(turn, slabt[s, h]).astype(BF16)

        def body(j, carry):
            at = 2 * s + j
            rows = sel[at, 1:2, 0:PAD]
            live = sel[at, 4:5, 0:PAD].astype(F32)
            for h in range(2):
                oht[h] = onehot(quarter, (2 * xh + h) * quarter, rows)
            target = dot(slabt[s, 0], oht[0]) + dot(slabt[s, 1], oht[1])
            positive = jnp.sum(qt[at].astype(F32) * target, axis=0, keepdims=True)
            positive_grad = -live * jax.nn.sigmoid(-positive)
            weight = live * (negs**-0.5)

            def part(i, carry):
                h, at_row = i // (quarter // chunk), lax.rem(i, quarter // chunk) * chunk
                here = pl.ds(pl.multiple_of(at_row, chunk), chunk)
                scores = dot(slab[h, here, :], qt[at])
                times = cnt[at, h, here, :]
                times = jnp.concatenate([times] * (PAD // 128), axis=1)
                grad = (jax.nn.sigmoid(scores) * (times * weight)).astype(BF16)
                ngm[h, here, :] = grad
                mark = oht[h, here, :].astype(F32)
                cm[at, h, here, :] = (grad.astype(F32) + mark * positive_grad).astype(BF16)
                return carry

            lax.fori_loop(0, 2 * (quarter // chunk), part, 0)
            grad = positive_grad * target + dot(slabt[s, 0], ngm[0]) + dot(slabt[s, 1], ngm[1])
            high = grad.astype(BF16)
            low = (grad - high.astype(F32)).astype(BF16)
            qhi[at] = high
            qlo[at] = low
            vectors = svt[at]
            main = dot_nt(vectors, qhi[at, 0:384]) + dot_nt(vectors, qlo[at, 0:384])
            rest = dot_nt(qhi[at, 384:width], vectors) + dot_nt(qlo[at, 384:width], vectors)
            rest = jnp.concatenate([rest, jnp.zeros((16, PAD - width), F32)], axis=1)
            second = sel[at, 3:4, 0:128].astype(F32).reshape(1, 1, 128)
            n = width // 16
            for k, share in ((0, 1.0 - second), (1, second)):
                for t in range(3):
                    tiles = main[:, 128 * t : 128 * t + 128].reshape(n, 16, 128)
                    acc[k, n * t : n * t + n] += tiles * share
                for t in range(4):
                    acc[k, 3 * n + t] += rest[:, 128 * t : 128 * t + 128] * share[0]
            return carry

        lax.fori_loop(0, 2, body, 0)

    queries(0)
    forwards = [forward(0)]
    queries(1)
    forwards.append(forward(1))
    forwards[0].wait_recv()
    score(0)
    forwards[1].wait_recv()
    score(1)

    copy0 = send(acc.at[1 - core], acc_in, ar0_s, ar0_r, sibling)

    def target_sums(i, carry):
        s, h = i // 2, lax.rem(i, 2)
        tsum[s, h] = dot_nt(qt[2 * s], cm[2 * s, h]) + dot_nt(qt[2 * s + 1], cm[2 * s + 1, h])
        return carry

    lax.fori_loop(0, 4, target_sums, 0)
    tx_copies = [
        send(tsum.at[s, 1 - core], tsum_in.at[s], tx_s.at[s], tx_r.at[s], sibling)
        for s in range(2)
    ]

    copy0.wait_recv()
    red[...] = acc[core] + acc_in[...]
    r1[0, x] = red[pl.ds(10 * x, 10)]
    r1[1, y] = red[pl.ds(40 + 10 * y, 10)]
    copies1 = []
    for k in range(1, 4):
        copies1.append(
            send(red.at[pl.ds(10 * x_at(k), 10)], r1.at[0, x], ar1_s.at[0, k - 1], ar1_r.at[0, k - 1], along_x(k))
        )
        copies1.append(
            send(red.at[pl.ds(40 + 10 * y_at(k), 10)], r1.at[1, y], ar1_s.at[1, k - 1], ar1_r.at[1, k - 1], along_y(k))
        )

    def source_vectors(at, carry):
        turned = operator(rel, at)
        sgt[at] = (dot(turned, qhi[at]) + dot(turned, qlo[at])).astype(BF16)
        return carry

    lax.fori_loop(0, 4, source_vectors, 0)

    def source_sums(q, carry):
        total = dot_nt(sgt[0], ohs[0, q])
        for at in range(1, 4):
            total += dot_nt(sgt[at], ohs[at, q])
        ssum[q // 2, lax.rem(q, 2)] = total
        return carry

    lax.fori_loop(0, 4, source_sums, 0)
    sx_copies = [
        send(ssum.at[h, 1 - core], ssum_in.at[h], sx_s.at[h], sx_r.at[h], sibling)
        for h in range(2)
    ]

    for copy in copies1:
        copy.wait_recv()
    for h in range(2):
        s1[h, 0:10] = (r1[h, 0] + r1[h, 1]) + (r1[h, 2] + r1[h, 3])
    r2[0, y] = s1[0, pl.ds(3 * y, 3)]
    r2[1, x] = s1[1, pl.ds(3 * x, 3)]
    copies2 = []
    for k in range(1, 4):
        copies2.append(
            send(s1.at[0, pl.ds(3 * y_at(k), 3)], r2.at[0, y], ar2_s.at[0, k - 1], ar2_r.at[0, k - 1], along_y(k))
        )
        copies2.append(
            send(s1.at[1, pl.ds(3 * x_at(k), 3)], r2.at[1, x], ar2_s.at[1, k - 1], ar2_r.at[1, k - 1], along_x(k))
        )

    ret_copies = []
    for s in range(2):
        tx_copies[s].wait_recv()
        ret[s] = (tsum[s, core] + tsum_in[s]).astype(BF16)
        ret_copies.append(
            send(ret.at[s], ret_in.at[s], ret_s.at[s], ret_r.at[s], along_blk(-(s + 1)))
        )

    for copy in copies2:
        copy.wait_recv()
    for h in range(2):
        s2[3 * h : 3 * h + 3] = (r2[h, 0] + r2[h, 1]) + (r2[h, 2] + r2[h, 3])
    r3[z] = s2[z]
    copies3 = [
        send(s2.at[z_at(k)], r3.at[z], ar3_s.at[k - 1], ar3_r.at[k - 1], along_z(k))
        for k in range(1, n_z)
    ]

    for copy in sx_copies:
        copy.wait_recv()
    half[...] = (ssum[1 - xh, core] + ssum_in[1 - xh]).astype(BF16)
    sy_copy = send(half, half_in, sy_s, sy_r, mate)

    for copy in copies3:
        copy.wait_recv()
    total = r3[0]
    for k in range(1, n_z):
        total += r3[k]
    g3[z] = total.astype(BF16)
    copies = [
        send(g3.at[z], g3.at[z], ag3_s.at[k - 1], ag3_r.at[k - 1], along_z(k))
        for k in range(1, n_z)
    ]
    sends = list(copies)
    for copy in copies:
        copy.wait_recv()
    g2[0, y] = g3[0:3]
    g2[1, x] = g3[3:6]
    copies = []
    for k in range(1, 4):
        copies.append(send(g2.at[0, y], g2.at[0, y], ag2_s.at[0, k - 1], ag2_r.at[0, k - 1], along_y(k)))
        copies.append(send(g2.at[1, x], g2.at[1, x], ag2_s.at[1, k - 1], ag2_r.at[1, k - 1], along_x(k)))
    sends += copies
    for copy in copies:
        copy.wait_recv()
    for h, at in ((0, x), (1, y)):
        for k in range(3):
            g1[h, at, 3 * k : 3 * k + 3] = g2[h, k]
        g1[h, at, 9] = g2[h, 3, 0]
    copies = []
    for k in range(1, 4):
        copies.append(send(g1.at[0, x], g1.at[0, x], ag1_s.at[0, k - 1], ag1_r.at[0, k - 1], along_x(k)))
        copies.append(send(g1.at[1, y], g1.at[1, y], ag1_s.at[1, k - 1], ag1_r.at[1, k - 1], along_y(k)))
    sends += copies

    sy_copy.wait_recv()
    for copy in ret_copies:
        copy.wait_recv()
    total = (ssum[xh, core] + ssum_in[xh]) + half_in[...].astype(F32)
    total = total + (ret_in[0].astype(F32) + ret_in[1].astype(F32))
    total = jnp.concatenate([total, jnp.zeros((PAD - width, quarter), F32)], axis=0)
    ent_out[...] = total.T[:, :width]

    for copy in copies:
        copy.wait_recv()
    copy = send(g1, g_other, ag0_s, ag0_r, sibling)
    sends.append(copy)

    def write(k, tiles):
        n = width // 16
        for t in range(3):
            rel_out[k, :, 128 * t : 128 * t + 128] = (
                tiles[n * t : n * t + n].astype(F32).reshape(width, 128)
            )
        rest = jnp.concatenate([tiles[3 * n + t].astype(F32) for t in range(4)], axis=1)
        rest = jnp.concatenate([rest, jnp.zeros((112, PAD), F32)], axis=0)
        rel_out[k, :, 384:width] = rest.T[:width, : width - 384]

    write(core, g1[...].reshape(TILES, 16, 128))
    copy.wait_recv()
    write(1 - core, g_other[...].reshape(TILES, 16, 128))

    for copy in slab_copies + forwards + [copy0, sy_copy]:
        copy.wait_send()
    for copy in tx_copies + copies1 + copies2 + copies3 + sx_copies + ret_copies + sends:
        copy.wait_send()


def on_device(n_y, n_z, embeddings, relations, *lists):
    rows, width = embeddings.shape
    quarter = rows // 4
    span = lists[0].shape[1] // 2
    negs = lists[2].shape[2]
    dma = pltpu.SemaphoreType.DMA
    vmem, smem = pl.BlockSpec(memory_space=pltpu.VMEM), pl.BlockSpec(memory_space=pltpu.SMEM)

    def buffer(*shape, kind=F32):
        return pltpu.VMEM(shape, kind)

    scratch = [
        buffer(4, width, quarter, kind=BF16),
        buffer(2, width, width, kind=BF16),
        buffer(2, 8, 1024, kind=I32),
        buffer(4, 8, 1024, kind=I32),
        buffer(4, 8, 1024, kind=I32),
        buffer(4, 4, quarter, PAD, kind=BF16),
        buffer(4, width, PAD, kind=BF16),
        buffer(4, width, PAD, kind=BF16),
        buffer(4, 2, quarter, 128),
        buffer(2, 2, width, quarter, kind=BF16),
        buffer(2, quarter, width, kind=BF16),
        buffer(2, quarter, PAD, kind=BF16),
        buffer(2, quarter, PAD, kind=BF16),
        buffer(4, 2, quarter, PAD, kind=BF16),
        buffer(4, width, PAD, kind=BF16),
        buffer(4, width, PAD, kind=BF16),
        buffer(4, width, PAD, kind=BF16),
        buffer(2, TILES, 16, 128),
        buffer(TILES, 16, 128),
        buffer(TILES, 16, 128),
        buffer(2, 4, 10, 16, 128),
        buffer(2, 12, 16, 128),
        buffer(2, 4, 3, 16, 128),
        buffer(8, 16, 128),
        buffer(8, 16, 128),
        buffer(8, 16, 128, kind=BF16),
        buffer(2, 4, 3, 16, 128, kind=BF16),
        buffer(2, 4, 10, 16, 128, kind=BF16),
        buffer(2, 4, 10, 16, 128, kind=BF16),
        buffer(2, 2, width, quarter),
        buffer(2, width, quarter),
        buffer(2, width, quarter, kind=BF16),
        buffer(2, width, quarter, kind=BF16),
        buffer(2, 2, width, quarter),
        buffer(2, width, quarter),
        buffer(width, quarter, kind=BF16),
        buffer(width, quarter, kind=BF16),
    ]
    for shape in (
        (3,), (2,), (2,), None, (2, 3), (2, 3), (n_z - 1,),
        (n_z - 1,), (2, 3), (2, 3), None, (2,), (2,), (2,), None,
    ):
        scratch += [dma if shape is None else dma(shape)] * 2
    return pl.pallas_call(
        functools.partial(kernel, n_y, n_z, span, negs),
        out_shape=(
            jax.ShapeDtypeStruct((quarter, width), F32),
            jax.ShapeDtypeStruct(relations.shape, F32),
        ),
        in_specs=[vmem] * 5 + [smem] * 2,
        out_specs=(vmem, vmem),
        scratch_shapes=scratch,
        compiler_params=pltpu.CompilerParams(
            collective_id=0, has_side_effects=True, vmem_limit_bytes=56 * 2**20
        ),
    )(embeddings, relations, *lists)


def solution(mesh):
    n_y = 4
    n_z = mesh.shape["blk"] // (2 * n_y)
    return jax.shard_map(
        functools.partial(on_device, n_y, n_z),
        mesh=mesh,
        in_specs=(
            P("blk", None),
            P(),
            P(None, ("blk", "rep")),
            P(None, ("blk", "rep")),
            P(None, ("blk", "rep"), None),
            P(None, ("blk", "rep")),
            P(None, ("blk", "rep")),
        ),
        out_specs=(P(("blk", "rep"), None), P()),
        check_vma=False,
    )
```

```python
import functools

import jax
import jax.numpy as jnp
from jax import lax
from jax.experimental import pallas as pl
from jax.experimental.pallas import tpu as pltpu
from jax.sharding import PartitionSpec as P

MESH = pl.DeviceIdType.MESH
F32, BF16, I32 = jnp.float32, jnp.bfloat16, jnp.int32
PAD = 512
TILES = 80


def dot(a, b):
    return lax.dot_general(a, b, (((1,), (0,)), ((), ())), preferred_element_type=F32)


def dot_nt(a, b):
    return lax.dot_general(a, b, (((1,), (1,)), ((), ())), preferred_element_type=F32)


def eye(n):
    return (
        lax.broadcasted_iota(I32, (n, n), 0) == lax.broadcasted_iota(I32, (n, n), 1)
    ).astype(F32).astype(BF16)


def onehot(rows, base, index):
    shape = (rows, index.shape[1])
    return (lax.broadcasted_iota(I32, shape, 0) + base == index).astype(F32).astype(BF16)


def kernel(
    n_y, n_z, span, negs,
    emb, rel, src, tgt, neg, srel, ecnt,
    ent_out, rel_out,
    opt, raw, lists, sel, ohs, svt, qt, cnt, slabt, slab, oht, ngm, pgs, qhl, sgt,
    acc, acc_in, red, r1, s1, r2, zx, g2, g1, g_other,
    tsum, tsum_in, ret, ret_in, ssum, ssum_in, half, half_in,
    idx_s, idx_r, slab_s, slab_r, fwd_s, fwd_r, ar0_s, ar0_r, ar1_s, ar1_r, ar2_s, ar2_r, ar3_s, ar3_r,
    ag2_s, ag2_r, ag1_s, ag1_r, ag0_s, ag0_r, tx_s, tx_r, ret_s, ret_r, sx_s, sx_r, sy_s, sy_r,
):
    width = emb.shape[0]
    n_blk = 2 * n_y * n_z
    quarter = emb.shape[1] // 4
    b, r = lax.axis_index("blk"), lax.axis_index("rep")
    xh, core = r // 2, lax.rem(r, 2)
    xl, y, z = lax.rem(b, 2), lax.rem(b // 2, n_y), b // (2 * n_y)
    x = xh * 2 + xl
    sibling = (b, xh * 2 + 1 - core)
    mate = (b, (1 - xh) * 2 + core)

    def along_blk(k):
        return (lax.rem(b + k + n_blk, n_blk), r)

    def along_rep(k):
        return (b, lax.rem(r + k, 4))

    def x_at(k):
        return lax.rem(x + k, 4)

    def y_at(k):
        return lax.rem(y + k, n_y)

    def z_at(k):
        return lax.rem(z + k, n_z)

    def along_x(k):
        there = x_at(k)
        return ((z * n_y + y) * 2 + lax.rem(there, 2), (there // 2) * 2 + core)

    def along_y(k):
        return ((z * n_y + y_at(k)) * 2 + xl, r)

    def along_z(k):
        return ((z_at(k) * n_y + y) * 2 + xl, r)

    def send(source, target, sent, received, device):
        copy = pltpu.make_async_remote_copy(
            src_ref=source, dst_ref=target, send_sem=sent, recv_sem=received,
            device_id=device, device_id_type=MESH,
        )
        copy.start()
        return copy

    barrier = pltpu.get_barrier_semaphore()
    peers = [along_blk(k) for k in (1, 2, -1, -2)] + [along_rep(k) for k in (1, 2, 3)]
    peers += [along_x(k) for k in (1, 2, 3)] + [along_y(k) for k in range(1, n_y)]
    peers += [along_z(k) for k in range(1, n_z)]
    for peer in peers:
        pl.semaphore_signal(barrier, inc=1, device_id=peer, device_id_type=MESH)

    lane = lax.broadcasted_iota(I32, (8, 1024), 1)
    row = lax.broadcasted_iota(I32, (8, 1024), 0)
    raw[...] = jnp.zeros(raw.shape, I32)
    raw[0, 0:2, 0 : 2 * span] = src[...]
    raw[0, 2:4, 0 : 2 * span] = tgt[...]
    for s in range(2):
        raw[1, 2 * s : 2 * s + 2, 0:negs] = neg[s]
    edges = raw[0]
    second = pltpu.roll(edges, PAD - span, 1)
    edges = jnp.where(lane < PAD, edges, second)
    negatives = raw[1]
    packed = jnp.zeros((8, 1024), I32)
    for s in range(2):
        words = edges[s : s + 1] + edges[2 + s : 3 + s] * 65536
        packed = jnp.where(row == 4 * s, words, packed)
        words = negatives[2 * s : 2 * s + 1] + negatives[2 * s + 1 : 2 * s + 2] * 65536
        packed = jnp.where(row == 4 * s + 1, words, packed)
        for k in range(2):
            live = jnp.clip(ecnt[0, s] - k * span, 0, span)
            packed = jnp.where(row == 4 * s + 2 + k, srel[s, k] + live * 65536, packed)
    lists[r] = packed

    pl.semaphore_wait(barrier, len(peers))

    index_copies = [
        send(lists.at[r], lists.at[r], idx_s.at[k - 1], idx_r.at[k - 1], along_rep(k))
        for k in (1, 2, 3)
    ]
    slab_copies = [
        send(emb.at[:, pl.ds(pl.multiple_of(r * quarter, quarter), quarter)], slabt.at[s, core], slab_s.at[s], slab_r.at[s], along_blk(s + 1))
        for s in range(2)
    ]

    unit = eye(width)
    for k in range(2):
        opt[k] = dot_nt(unit, rel[k]).astype(BF16)
    s1[...] = jnp.zeros(s1.shape, F32)
    for copy in index_copies:
        copy.wait()

    for s in range(2):
        before = jnp.zeros((1, 1024), I32)
        edge_words = [jnp.zeros((1, PAD), I32) for j in range(2)]
        negative_words = [jnp.zeros((1, 1024), I32) for j in range(2)]
        meta_words = [jnp.zeros((1, 1024), I32) for j in range(2)]
        for d in range(4):
            rows = lists[d]
            for k in range(2):
                meta = rows[4 * s + 2 + k : 4 * s + 3 + k]
                alive = (meta >= 65536).astype(I32)
                both = rows[4 * s + 1 : 4 * s + 2]
                negative = (both & 65535) if k == 0 else (both >> 16)
                edge = rows[4 * s : 4 * s + 1, k * PAD : (k + 1) * PAD]
                for j in range(2):
                    mine = alive * (before == 2 * core + j).astype(I32)
                    edge_words[j] += edge * mine[:, :PAD]
                    negative_words[j] += negative * mine
                    meta_words[j] += meta * mine
                before = before + alive
        lane1 = lax.broadcasted_iota(I32, (1, 1024), 1)
        for j in range(2):
            valid = lane1[:, :PAD] < (meta_words[j][:, :PAD] >> 16)
            at = 2 * s + j
            sel[at, 0:1, 0:PAD] = jnp.where(valid, edge_words[j] & 65535, -1)
            sel[at, 1:2, 0:PAD] = jnp.where(valid, edge_words[j] >> 16, -1)
            sel[at, 2:3, :] = jnp.where(lane1 < negs, negative_words[j], -1)
            sel[at, 3:4, :] = meta_words[j] & 1
            sel[at, 4:5, 0:PAD] = valid.astype(I32)

    def operator(table, at):
        second = sel[at, 3:4, 0:width].astype(F32)
        return (
            table[0].astype(F32) * (1.0 - second) + table[1].astype(F32) * second
        ).astype(BF16)

    def queries(s):
        for j in range(2):
            at = 2 * s + j
            ohs[at] = onehot(4 * quarter, 0, sel[at, 0:1, 0:PAD])
            vectors = dot(emb[...], ohs[at]).astype(BF16)
            svt[at] = vectors
            qt[at] = dot(operator(opt, at), vectors).astype(BF16)
            times = dot(onehot(2 * quarter, 2 * xh * quarter, sel[at, 2:3, :]), jnp.ones((1024, 128), BF16))
            cnt[at] = times * (0.5 * negs**-0.5)

    def forward(s):
        slab_copies[s].wait_recv()
        return send(
            slabt.at[s, core], slabt.at[s, core], fwd_s.at[s], fwd_r.at[s], sibling
        )

    def score(s):
        turn = eye(quarter) * jnp.asarray(0.5, BF16)
        for h in range(2):
            slab[h * quarter : (h + 1) * quarter] = dot_nt(turn, slabt[s, h]).astype(BF16)
        turned = jnp.concatenate([slabt[s, 0], slabt[s, 1]], axis=1)
        mains, rests, seconds = [], [], []
        for j in range(2):
            at = 2 * s + j
            oht[at] = onehot(2 * quarter, 2 * xh * quarter, sel[at, 1:2, 0:PAD])
            query = qt[at]
            target = dot(turned, oht[at])
            positive = jnp.sum(query.astype(F32) * target, axis=0, keepdims=True)
            positive_grad = -sel[at, 4:5, 0:PAD].astype(F32) * jax.nn.sigmoid(-positive)
            pgs[at, 0:1] = positive_grad
            for i in range(0, 2 * quarter, 128):
                bent = jnp.tanh(dot(slab[i : i + 128], query))
                times = jnp.concatenate([cnt[at, i : i + 128]] * (PAD // 128), axis=1)
                ngm[at, i : i + 128] = (times * bent + times).astype(BF16)
            grad = positive_grad * target + dot(turned, ngm[at])
            high = grad.astype(BF16)
            qhl[at, :, 0:PAD] = high
            qhl[at, :, PAD:] = (grad - high.astype(F32)).astype(BF16)
            vectors = jnp.concatenate([svt[at]] * 2, axis=1)
            mains.append(dot_nt(vectors, qhl[at, 0:384]))
            rest = dot_nt(qhl[at, 384:width], vectors)
            rests.append(jnp.concatenate([rest, jnp.zeros((16, PAD - width), F32)], axis=1))
            seconds.append(sel[at, 3:4, 0:128].astype(F32))
        n = width // 16
        for k in range(2):
            shares = [second if k else 1.0 - second for second in seconds]
            for t in range(3):
                tiles = sum(
                    main[:, 128 * t : 128 * t + 128] * share for main, share in zip(mains, shares)
                ).reshape(n, 16, 128)
                acc[k, n * t : n * t + n] = tiles if s == 0 else acc[k, n * t : n * t + n] + tiles
            for t in range(4):
                tile = sum(
                    rest[:, 128 * t : 128 * t + 128] * share for rest, share in zip(rests, shares)
                )
                acc[k, 3 * n + t] = tile if s == 0 else acc[k, 3 * n + t] + tile
            if s == 0:
                acc[k, 3 * n + 4] = jnp.zeros((16, 128), F32)

    queries(0)
    queries(1)
    forwards = [forward(0)]
    forwards[0].wait_recv()
    score(0)
    forwards.append(forward(1))
    forwards[1].wait_recv()
    score(1)

    copy0 = send(acc.at[1 - core], acc_in, ar0_s, ar0_r, sibling)
    copy0.wait_recv()
    red[...] = acc[core] + acc_in[...]
    r1[0, x] = red[pl.ds(10 * x, 10)]
    r1[1, y] = red[pl.ds(40 + 10 * y, 10)]
    copies1 = []
    for k in (2, 1, 3):
        copies1.append(
            send(red.at[pl.ds(10 * x_at(k), 10)], r1.at[0, x], ar1_s.at[0, k - 1], ar1_r.at[0, k - 1], along_x(k))
        )
        copies1.append(
            send(red.at[pl.ds(40 + 10 * y_at(k), 10)], r1.at[1, y], ar1_s.at[1, k - 1], ar1_r.at[1, k - 1], along_y(k))
        )

    for s in range(2):
        positives = [(pgs[at, 0:1] * qt[at].astype(F32)).astype(BF16) for at in (2 * s, 2 * s + 1)]
        left = jnp.concatenate([qt[2 * s], qt[2 * s + 1]] + positives, axis=1)
        for h in range(2):
            rows = slice(h * quarter, (h + 1) * quarter)
            parts = [ngm[2 * s, rows], ngm[2 * s + 1, rows], oht[2 * s, rows], oht[2 * s + 1, rows]]
            tsum[s, h] = dot_nt(left, jnp.concatenate(parts, axis=1))
    tx_copies = [
        send(tsum.at[s, 1 - core], tsum_in.at[s], tx_s.at[s], tx_r.at[s], sibling)
        for s in range(2)
    ]

    for at in range(4):
        turned = operator(rel, at)
        both = jnp.concatenate([qhl[at, :, 0:PAD], qhl[at, :, PAD:]], axis=0)
        sgt[at] = dot(jnp.concatenate([turned, turned], axis=1), both).astype(BF16)

    left = jnp.concatenate([sgt[at] for at in range(4)], axis=1)
    for q in range(4):
        rows = slice(q * quarter, (q + 1) * quarter)
        ssum[q // 2, q % 2] = dot_nt(left, jnp.concatenate([ohs[at, rows] for at in range(4)], axis=1))
    sx_copies = [
        send(ssum.at[h, 1 - core], ssum_in.at[h], sx_s.at[h], sx_r.at[h], sibling)
        for h in range(2)
    ]

    for copy in copies1:
        copy.wait_recv()
    for h in range(2):
        s1[h, 0:10] = (r1[h, 0] + r1[h, 1]) + (r1[h, 2] + r1[h, 3])
    r2[0, y] = s1[0, pl.ds(3 * y, 3)]
    r2[1, x] = s1[1, pl.ds(3 * x, 3)]
    copies2 = []
    for k in range(1, 4):
        copies2.append(
            send(s1.at[0, pl.ds(3 * y_at(k), 3)], r2.at[0, y], ar2_s.at[0, k - 1], ar2_r.at[0, k - 1], along_y(k))
        )
        copies2.append(
            send(s1.at[1, pl.ds(3 * x_at(k), 3)], r2.at[1, x], ar2_s.at[1, k - 1], ar2_r.at[1, k - 1], along_x(k))
        )

    for copy in copies2:
        copy.wait_recv()
    for h in range(2):
        total = (r2[h, 0] + r2[h, 1]) + (r2[h, 2] + r2[h, 3])
        zx[z, 3 * h : 3 * h + 3] = total.astype(BF16)
    copies3 = [
        send(zx.at[z], zx.at[z], ar3_s.at[k - 1], ar3_r.at[k - 1], along_z(k))
        for k in sorted(range(1, n_z), key=lambda k: -min(k, n_z - k))
    ]

    for copy in sx_copies:
        copy.wait_recv()
    half[...] = (ssum[1 - xh, core] + ssum_in[1 - xh]).astype(BF16)
    sy_copy = send(half, half_in, sy_s, sy_r, mate)
    ret_copies = []
    for s in range(2):
        tx_copies[s].wait_recv()
        ret[s] = (tsum[s, core] + tsum_in[s]).astype(BF16)
        ret_copies.append(
            send(ret.at[s], ret_in.at[s], ret_s.at[s], ret_r.at[s], along_blk(-(s + 1)))
        )

    for copy in copies3:
        copy.wait_recv()
    total = zx[0].astype(F32)
    for k in range(1, n_z):
        total += zx[k].astype(F32)
    total = total.astype(BF16)
    g2[0, y] = total[0:3]
    g2[1, x] = total[3:6]
    copies = []
    for k in (2, 1, 3):
        copies.append(send(g2.at[0, y], g2.at[0, y], ag2_s.at[0, k - 1], ag2_r.at[0, k - 1], along_y(k)))
        copies.append(send(g2.at[1, x], g2.at[1, x], ag2_s.at[1, k - 1], ag2_r.at[1, k - 1], along_x(k)))
    sends = list(copies)
    for copy in copies:
        copy.wait_recv()
    for h, at in ((0, x), (1, y)):
        for k in range(3):
            g1[h, at, 3 * k : 3 * k + 3] = g2[h, k]
        g1[h, at, 9] = g2[h, 3, 0]
    copies = []
    for k in (2, 1, 3):
        copies.append(send(g1.at[0, x], g1.at[0, x], ag1_s.at[0, k - 1], ag1_r.at[0, k - 1], along_x(k)))
        copies.append(send(g1.at[1, y], g1.at[1, y], ag1_s.at[1, k - 1], ag1_r.at[1, k - 1], along_y(k)))
    sends += copies
    handed = [
        send(g1.at[h, at], g_other.at[h, at], ag0_s.at[h, 0], ag0_r.at[h, 0], sibling)
        for h, at in ((0, x), (1, y))
    ]

    sy_copy.wait_recv()
    for copy in ret_copies:
        copy.wait_recv()
    total = (ssum[xh, core] + ssum_in[xh]) + half_in[...].astype(F32)
    total = total + (ret_in[0].astype(F32) + ret_in[1].astype(F32))
    ent_out[...] = total

    for i, k in ((1, 1), (2, 3), (0, 2)):
        copies[2 * i].wait_recv()
        copies[2 * i + 1].wait_recv()
        for h, at in ((0, x_at(4 - k)), (1, y_at(4 - k))):
            handed.append(
                send(g1.at[h, at], g_other.at[h, at], ag0_s.at[h, k], ag0_r.at[h, k], sibling)
            )

    def write(k, tiles):
        n = width // 16
        for t in range(3):
            rel_out[k, :, 128 * t : 128 * t + 128] = tiles[n * t : n * t + n].reshape(width, 128)
        rest = jnp.concatenate([tiles[3 * n + t].astype(F32) for t in range(4)], axis=1)
        rest = jnp.concatenate([rest, jnp.zeros((112, PAD), F32)], axis=0)
        rel_out[k, :, 384:width] = rest.T[:width, : width - 384].astype(BF16)

    write(core, g1[...].reshape(TILES, 16, 128))
    for copy in handed:
        copy.wait_recv()
    write(1 - core, g_other[...].reshape(TILES, 16, 128))

    for copy in slab_copies + forwards + [copy0, sy_copy] + handed + sends:
        copy.wait_send()
    for copy in tx_copies + copies1 + copies2 + copies3 + sx_copies + ret_copies:
        copy.wait_send()


def on_device(n_y, n_z, embeddings, relations, *lists):
    rows, width = embeddings.shape
    quarter = rows // 4
    span = lists[0].shape[1] // 2
    negs = lists[2].shape[2]
    dma = pltpu.SemaphoreType.DMA
    vmem, smem = pl.BlockSpec(memory_space=pltpu.VMEM), pl.BlockSpec(memory_space=pltpu.SMEM)

    def buffer(*shape, kind=F32):
        return pltpu.VMEM(shape, kind)

    scratch = [
        buffer(2, width, width, kind=BF16),
        buffer(2, 8, 1024, kind=I32),
        buffer(4, 8, 1024, kind=I32),
        buffer(4, 8, 1024, kind=I32),
        buffer(4, rows, PAD, kind=BF16),
        buffer(4, width, PAD, kind=BF16),
        buffer(4, width, PAD, kind=BF16),
        buffer(4, rows // 2, 128),
        buffer(2, 2, width, quarter, kind=BF16),
        buffer(rows // 2, width, kind=BF16),
        buffer(4, rows // 2, PAD, kind=BF16),
        buffer(4, rows // 2, PAD, kind=BF16),
        buffer(4, 8, PAD),
        buffer(4, width, 2 * PAD, kind=BF16),
        buffer(4, width, PAD, kind=BF16),
        buffer(2, TILES, 16, 128),
        buffer(TILES, 16, 128),
        buffer(TILES, 16, 128),
        buffer(2, 4, 10, 16, 128),
        buffer(2, 12, 16, 128),
        buffer(2, 4, 3, 16, 128),
        buffer(n_z, 6, 16, 128, kind=BF16),
        buffer(2, 4, 3, 16, 128, kind=BF16),
        buffer(2, 4, 10, 16, 128, kind=BF16),
        buffer(2, 4, 10, 16, 128, kind=BF16),
        buffer(2, 2, width, quarter),
        buffer(2, width, quarter),
        buffer(2, width, quarter, kind=BF16),
        buffer(2, width, quarter, kind=BF16),
        buffer(2, 2, width, quarter),
        buffer(2, width, quarter),
        buffer(width, quarter, kind=BF16),
        buffer(width, quarter, kind=BF16),
    ]
    for shape in (
        (3,), (2,), (2,), None, (2, 3), (2, 3), (n_z - 1,),
        (2, 3), (2, 3), (2, 4), (2,), (2,), (2,), None,
    ):
        scratch += [dma if shape is None else dma(shape)] * 2
    entity, relation = pl.pallas_call(
        functools.partial(kernel, n_y, n_z, span, negs),
        out_shape=(
            jax.ShapeDtypeStruct((width, quarter), F32),
            jax.ShapeDtypeStruct(relations.shape, BF16),
        ),
        in_specs=[vmem] * 5 + [smem] * 2,
        out_specs=(vmem, vmem),
        scratch_shapes=scratch,
        compiler_params=pltpu.CompilerParams(
            collective_id=0, has_side_effects=True, vmem_limit_bytes=56 * 2**20
        ),
    )(embeddings.T, relations, *lists[:-1], lists[-1].T)
    return entity.T, relation.astype(F32)


def solution(mesh):
    n_y = 4
    n_z = mesh.shape["blk"] // (2 * n_y)
    return jax.shard_map(
        functools.partial(on_device, n_y, n_z),
        mesh=mesh,
        in_specs=(
            P("blk", None),
            P(),
            P(None, ("blk", "rep")),
            P(None, ("blk", "rep")),
            P(None, ("blk", "rep"), None),
            P(None, ("blk", "rep")),
            P(None, ("blk", "rep")),
        ),
        out_specs=(P(("blk", "rep"), None), P()),
        check_vma=False,
    )
```

```python
import functools

import jax
import jax.numpy as jnp
from jax import lax
from jax.experimental import pallas as pl
from jax.experimental.pallas import tpu as pltpu
from jax.sharding import PartitionSpec as P

MESH = pl.DeviceIdType.MESH
F32, BF16, I32 = jnp.float32, jnp.bfloat16, jnp.int32
PAD = 512
TILES = 80


def dot(a, b):
    return lax.dot_general(a, b, (((1,), (0,)), ((), ())), preferred_element_type=F32)


def dot_nt(a, b):
    return lax.dot_general(a, b, (((1,), (1,)), ((), ())), preferred_element_type=F32)


def eye(n):
    return (
        lax.broadcasted_iota(I32, (n, n), 0) == lax.broadcasted_iota(I32, (n, n), 1)
    ).astype(F32).astype(BF16)


def onehot(rows, base, index):
    shape = (rows, index.shape[1])
    return (lax.broadcasted_iota(I32, shape, 0) + base == index).astype(F32).astype(BF16)


def kernel(
    n_y, n_z, span, negs,
    emb_hbm, rel_hbm, src, tgt, neg, srel, ecnt,
    ent_out, rel_out,
    emb, rel, opt, raw, lists, sel, ohs, svt, qt, cnt, slabt, slab, oht, ngm, pgs, qhl, sgt,
    acc, acc_last, acc_in, red, red_out, r1, s1, r2, zx, g2, g1, g_other,
    tsum, tsum_in, ret, ret_in, ssum, ssum_in, half, half_in,
    load, idx_s, idx_r, slab_s, slab_r, fwd_s, fwd_r, ar0_s, ar0_r, ar1_s, ar1_r, ar2_s, ar2_r, ar3_s, ar3_r,
    ag2_s, ag2_r, ag1_s, ag1_r, ag0_s, ag0_r, tx_s, tx_r, ret_s, ret_r, sx_s, sx_r, sy_s, sy_r,
):
    width = emb.shape[0]
    n_blk = 2 * n_y * n_z
    quarter = emb.shape[1] // 4
    b, r = lax.axis_index("blk"), lax.axis_index("rep")
    xh, core = r // 2, lax.rem(r, 2)
    xl, y, z = lax.rem(b, 2), lax.rem(b // 2, n_y), b // (2 * n_y)
    x = xh * 2 + xl
    sibling = (b, xh * 2 + 1 - core)
    mate = (b, (1 - xh) * 2 + core)

    def along_blk(k):
        return (lax.rem(b + k + n_blk, n_blk), r)

    def along_rep(k):
        return (b, lax.rem(r + k, 4))

    def x_at(k):
        return lax.rem(x + k, 4)

    def y_at(k):
        return lax.rem(y + k, n_y)

    def z_at(k):
        return lax.rem(z + k, n_z)

    def along_x(k):
        there = x_at(k)
        return ((z * n_y + y) * 2 + lax.rem(there, 2), (there // 2) * 2 + core)

    def along_y(k):
        return ((z * n_y + y_at(k)) * 2 + xl, r)

    def along_z(k):
        return ((z_at(k) * n_y + y) * 2 + xl, r)

    def send(source, target, sent, received, device):
        copy = pltpu.make_async_remote_copy(
            src_ref=source, dst_ref=target, send_sem=sent, recv_sem=received,
            device_id=device, device_id_type=MESH,
        )
        copy.start()
        return copy

    barrier = pltpu.get_barrier_semaphore()
    peers = [along_blk(k) for k in (1, 2, -1, -2)] + [along_rep(k) for k in (1, 2, 3)]
    peers += [along_x(k) for k in (1, 2, 3)] + [along_y(k) for k in range(1, n_y)]
    peers += [along_z(k) for k in range(1, n_z)]
    for peer in peers:
        pl.semaphore_signal(barrier, inc=1, device_id=peer, device_id_type=MESH)

    loads = [
        pltpu.make_async_copy(emb_hbm, emb, load.at[0]),
        pltpu.make_async_copy(rel_hbm, rel, load.at[1]),
    ]
    for copy in loads:
        copy.start()
    lane = lax.broadcasted_iota(I32, (8, 1024), 1)
    row = lax.broadcasted_iota(I32, (8, 1024), 0)
    raw[...] = jnp.zeros(raw.shape, I32)
    raw[0, 0:2, 0 : 2 * span] = src[...]
    raw[0, 2:4, 0 : 2 * span] = tgt[...]
    for s in range(2):
        raw[1, 2 * s : 2 * s + 2, 0:negs] = neg[s]
    edges = raw[0]
    second = pltpu.roll(edges, PAD - span, 1)
    edges = jnp.where(lane < PAD, edges, second)
    negatives = raw[1]
    packed = jnp.zeros((8, 1024), I32)
    for s in range(2):
        words = edges[s : s + 1] + edges[2 + s : 3 + s] * 65536
        packed = jnp.where(row == 4 * s, words, packed)
        words = negatives[2 * s : 2 * s + 1] + negatives[2 * s + 1 : 2 * s + 2] * 65536
        packed = jnp.where(row == 4 * s + 1, words, packed)
        for k in range(2):
            live = jnp.clip(ecnt[0, s] - k * span, 0, span)
            packed = jnp.where(row == 4 * s + 2 + k, srel[s, k] + live * 65536, packed)
    lists[r] = packed

    pl.semaphore_wait(barrier, len(peers))

    index_copies = [
        send(lists.at[r], lists.at[r], idx_s.at[k - 1], idx_r.at[k - 1], along_rep(k))
        for k in (2, 1, 3)
    ]
    here = pl.ds(pl.multiple_of(r * quarter, quarter), quarter)
    slab_copies = [
        send(emb_hbm.at[:, here], slabt.at[s, core], slab_s.at[s], slab_r.at[s], along_blk(s + 1))
        for s in range(2)
    ]

    for copy in loads:
        copy.wait()
    unit = eye(width)
    for k in range(2):
        opt[k] = dot_nt(unit, rel[k]).astype(BF16)
    s1[...] = jnp.zeros(s1.shape, F32)
    for copy in index_copies:
        copy.wait()

    for s in range(2):
        before = jnp.zeros((1, 1024), I32)
        edge_words = [jnp.zeros((1, PAD), I32) for j in range(2)]
        negative_words = [jnp.zeros((1, 1024), I32) for j in range(2)]
        meta_words = [jnp.zeros((1, 1024), I32) for j in range(2)]
        for d in range(4):
            rows = lists[d]
            for k in range(2):
                meta = rows[4 * s + 2 + k : 4 * s + 3 + k]
                alive = (meta >= 65536).astype(I32)
                both = rows[4 * s + 1 : 4 * s + 2]
                negative = (both & 65535) if k == 0 else (both >> 16)
                edge = rows[4 * s : 4 * s + 1, k * PAD : (k + 1) * PAD]
                for j in range(2):
                    mine = alive * (before == 2 * core + j).astype(I32)
                    edge_words[j] += edge * mine[:, :PAD]
                    negative_words[j] += negative * mine
                    meta_words[j] += meta * mine
                before = before + alive
        lane1 = lax.broadcasted_iota(I32, (1, 1024), 1)
        for j in range(2):
            valid = lane1[:, :PAD] < (meta_words[j][:, :PAD] >> 16)
            at = 2 * s + j
            sel[at, 0:1, 0:PAD] = jnp.where(valid, edge_words[j] & 65535, -1)
            sel[at, 1:2, 0:PAD] = jnp.where(valid, edge_words[j] >> 16, -1)
            sel[at, 2:3, :] = jnp.where(lane1 < negs, negative_words[j], -1)
            sel[at, 3:4, :] = meta_words[j] & 1
            sel[at, 4:5, 0:PAD] = valid.astype(I32)

    def operator(table, at):
        second = sel[at, 3:4, 0:width].astype(F32)
        return (
            table[0].astype(F32) * (1.0 - second) + table[1].astype(F32) * second
        ).astype(BF16)

    def queries(s):
        for j in range(2):
            at = 2 * s + j
            ohs[at] = onehot(4 * quarter, 0, sel[at, 0:1, 0:PAD])
            vectors = dot(emb[...], ohs[at]).astype(BF16)
            svt[at] = vectors
            qt[at] = dot(operator(opt, at), vectors).astype(BF16)
            times = dot(onehot(2 * quarter, 2 * xh * quarter, sel[at, 2:3, :]), jnp.ones((1024, 128), BF16))
            cnt[at] = times * (0.5 * negs**-0.5)

    def forward(s):
        slab_copies[s].wait_recv()
        return send(
            slabt.at[s, core], slabt.at[s, core], fwd_s.at[s], fwd_r.at[s], sibling
        )

    def score(s):
        turn = eye(quarter) * jnp.asarray(0.5, BF16)
        for h in range(2):
            slab[h * quarter : (h + 1) * quarter] = dot_nt(turn, slabt[s, h]).astype(BF16)
        turned = jnp.concatenate([slabt[s, 0], slabt[s, 1]], axis=1)
        mains, seconds = [], []
        for j in range(2):
            at = 2 * s + j
            oht[at] = onehot(2 * quarter, 2 * xh * quarter, sel[at, 1:2, 0:PAD])
            query = qt[at]
            target = dot(turned, oht[at])
            positive = jnp.sum(query.astype(F32) * target, axis=0, keepdims=True)
            positive_grad = -sel[at, 4:5, 0:PAD].astype(F32) * jax.nn.sigmoid(-positive)
            pgs[at, 0:1] = positive_grad
            bent = jnp.tanh(dot(slab[...], query))
            times = jnp.concatenate([cnt[at]] * (PAD // 128), axis=1)
            ngm[at] = (times * bent + times).astype(BF16)
            grad = positive_grad * target + dot(turned, ngm[at])
            high = grad.astype(BF16)
            qhl[at, :, 0:PAD] = high
            qhl[at, :, PAD:] = (grad - high.astype(F32)).astype(BF16)
            vectors = jnp.concatenate([svt[at]] * 2, axis=1)
            mains.append(dot_nt(vectors, qhl[at]))
            seconds.append(sel[at, 3:4, 0:128].astype(F32))
        return mains, seconds

    n = width // 16

    def accumulate(s, k, mains, seconds):
        first = jnp.where(k == 0, 1.0, 0.0)
        shares = [first + second * (1.0 - 2.0 * first) for second in seconds]
        for t in range(3):
            tiles = sum(
                main[:, 128 * t : 128 * t + 128] * share for main, share in zip(mains, shares)
            ).reshape(n, 16, 128)
            acc[k, n * t : n * t + n] = tiles if s == 0 else acc[k, n * t : n * t + n] + tiles
        last = sum(
            main[:, 384:width] * share[:, : width - 384] for main, share in zip(mains, shares)
        )
        last = jnp.concatenate([last, jnp.zeros((width, PAD - width), F32)], axis=1)
        if s == 0:
            acc_last[k] = last
            return
        last = acc_last[k] + last
        last = jnp.concatenate([last, jnp.zeros((PAD - width, 128), F32)], axis=0).T
        for t in range(4):
            acc[k, 3 * n + t] = last[:16, 128 * t : 128 * t + 128]
        acc[k, 3 * n + 4] = jnp.zeros((16, 128), F32)

    queries(0)
    queries(1)
    forwards = [forward(0)]
    forwards[0].wait_recv()
    found = score(0)
    for k in range(2):
        accumulate(0, k, *found)
    forwards.append(forward(1))
    forwards[1].wait_recv()
    found = score(1)
    accumulate(1, 1 - core, *found)
    copy0 = send(acc.at[1 - core], acc_in, ar0_s, ar0_r, sibling)
    accumulate(1, core, *found)
    copy0.wait_recv()
    red[...] = acc[core] + acc_in[...]
    red_out[...] = red[...].astype(BF16)
    copies1 = []
    for k in (2, 1, 3):
        copies1.append(
            send(red_out.at[pl.ds(10 * x_at(k), 10)], r1.at[0, k - 1], ar1_s.at[0, k - 1], ar1_r.at[0, k - 1], along_x(k))
        )
        copies1.append(
            send(red_out.at[pl.ds(40 + 10 * y_at(k), 10)], r1.at[1, k - 1], ar1_s.at[1, k - 1], ar1_r.at[1, k - 1], along_y(k))
        )

    for s in range(2):
        positives = [(pgs[at, 0:1] * qt[at].astype(F32)).astype(BF16) for at in (2 * s, 2 * s + 1)]
        left = jnp.concatenate([qt[2 * s], qt[2 * s + 1]] + positives, axis=1)
        for h in range(2):
            rows = slice(h * quarter, (h + 1) * quarter)
            parts = [ngm[2 * s, rows], ngm[2 * s + 1, rows], oht[2 * s, rows], oht[2 * s + 1, rows]]
            tsum[s, h] = dot_nt(left, jnp.concatenate(parts, axis=1))
    tx_copies = [
        send(tsum.at[s, 1 - core], tsum_in.at[s], tx_s.at[s], tx_r.at[s], sibling)
        for s in range(2)
    ]

    for at in range(4):
        turned = operator(rel, at)
        both = jnp.concatenate([qhl[at, :, 0:PAD], qhl[at, :, PAD:]], axis=0)
        sgt[at] = dot(jnp.concatenate([turned, turned], axis=1), both).astype(BF16)

    left = jnp.concatenate([sgt[at] for at in range(4)], axis=1)
    for q in range(4):
        rows = slice(q * quarter, (q + 1) * quarter)
        ssum[q // 2, q % 2] = dot_nt(left, jnp.concatenate([ohs[at, rows] for at in range(4)], axis=1))
    sx_copies = [
        send(ssum.at[h, 1 - core], ssum_in.at[h], sx_s.at[h], sx_r.at[h], sibling)
        for h in range(2)
    ]

    for copy in copies1:
        copy.wait_recv()
    for h, at in ((0, 10 * x), (1, 40 + 10 * y)):
        total = red[pl.ds(at, 10)]
        for k in range(3):
            total += r1[h, k].astype(F32)
        s1[h, 0:10] = total
    r2[0, y] = s1[0, pl.ds(3 * y, 3)]
    r2[1, x] = s1[1, pl.ds(3 * x, 3)]
    copies2 = []
    for k in range(1, 4):
        copies2.append(
            send(s1.at[0, pl.ds(3 * y_at(k), 3)], r2.at[0, y], ar2_s.at[0, k - 1], ar2_r.at[0, k - 1], along_y(k))
        )
        copies2.append(
            send(s1.at[1, pl.ds(3 * x_at(k), 3)], r2.at[1, x], ar2_s.at[1, k - 1], ar2_r.at[1, k - 1], along_x(k))
        )

    for copy in copies2:
        copy.wait_recv()
    for h in range(2):
        total = (r2[h, 0] + r2[h, 1]) + (r2[h, 2] + r2[h, 3])
        zx[z, 3 * h : 3 * h + 3] = total.astype(BF16)
    copies3 = [
        send(zx.at[z], zx.at[z], ar3_s.at[k - 1], ar3_r.at[k - 1], along_z(k))
        for k in sorted(range(1, n_z), key=lambda k: -min(k, n_z - k))
    ]

    for copy in sx_copies:
        copy.wait_recv()
    half[...] = (ssum[1 - xh, core] + ssum_in[1 - xh]).astype(BF16)
    sy_copy = send(half, half_in, sy_s, sy_r, mate)
    ret_copies = []
    for s in range(2):
        tx_copies[s].wait_recv()
        ret[s] = (tsum[s, core] + tsum_in[s]).astype(BF16)
        ret_copies.append(
            send(ret.at[s], ret_in.at[s], ret_s.at[s], ret_r.at[s], along_blk(-(s + 1)))
        )

    for copy in copies3:
        copy.wait_recv()
    total = zx[0].astype(F32)
    for k in range(1, n_z):
        total += zx[k].astype(F32)
    total = total.astype(BF16)
    g2[0, y] = total[0:3]
    g2[1, x] = total[3:6]
    copies = []
    for k in (2, 1, 3):
        copies.append(send(g2.at[0, y], g2.at[0, y], ag2_s.at[0, k - 1], ag2_r.at[0, k - 1], along_y(k)))
        copies.append(send(g2.at[1, x], g2.at[1, x], ag2_s.at[1, k - 1], ag2_r.at[1, k - 1], along_x(k)))
    sends = list(copies)
    for copy in copies:
        copy.wait_recv()
    for h, at in ((0, x), (1, y)):
        for k in range(3):
            g1[h, at, 3 * k : 3 * k + 3] = g2[h, k]
        g1[h, at, 9] = g2[h, 3, 0]
    copies = []
    for k in (2, 1, 3):
        copies.append(send(g1.at[0, x], g1.at[0, x], ag1_s.at[0, k - 1], ag1_r.at[0, k - 1], along_x(k)))
        copies.append(send(g1.at[1, y], g1.at[1, y], ag1_s.at[1, k - 1], ag1_r.at[1, k - 1], along_y(k)))
    sends += copies
    handed = [
        send(g1.at[h, at], g_other.at[h, at], ag0_s.at[h, 0], ag0_r.at[h, 0], sibling)
        for h, at in ((0, x), (1, y))
    ]

    sy_copy.wait_recv()
    for copy in ret_copies:
        copy.wait_recv()
    total = (ssum[xh, core] + ssum_in[xh]) + half_in[...].astype(F32)
    total = total + (ret_in[0].astype(F32) + ret_in[1].astype(F32))
    ent_out[...] = total

    for i, k in ((1, 1), (2, 3), (0, 2)):
        copies[2 * i].wait_recv()
        copies[2 * i + 1].wait_recv()
        for h, at in ((0, x_at(4 - k)), (1, y_at(4 - k))):
            handed.append(
                send(g1.at[h, at], g_other.at[h, at], ag0_s.at[h, k], ag0_r.at[h, k], sibling)
            )

    def write(k, tiles):
        for t in range(3):
            rel_out[k, :, 128 * t : 128 * t + 128] = tiles[n * t : n * t + n].reshape(width, 128)
        rest = jnp.concatenate([tiles[3 * n + t].astype(F32) for t in range(4)], axis=1)
        rest = jnp.concatenate([rest, jnp.zeros((112, PAD), F32)], axis=0)
        rel_out[k, :, 384:width] = rest.T[:width, : width - 384].astype(BF16)

    write(core, g1[...].reshape(TILES, 16, 128))
    for copy in handed:
        copy.wait_recv()
    write(1 - core, g_other[...].reshape(TILES, 16, 128))

    for copy in slab_copies + forwards + [copy0, sy_copy] + handed + sends:
        copy.wait_send()
    for copy in tx_copies + copies1 + copies2 + copies3 + sx_copies + ret_copies:
        copy.wait_send()


def hand_over(entity, relation, entity_out, relation_out):
    entity_out[...] = entity[...]
    relation_out[...] = relation[...].astype(F32)


def on_device(n_y, n_z, embeddings, relations, *lists):
    rows, width = embeddings.shape
    quarter = rows // 4
    span = lists[0].shape[1] // 2
    negs = lists[2].shape[2]
    dma = pltpu.SemaphoreType.DMA
    vmem, smem = pl.BlockSpec(memory_space=pltpu.VMEM), pl.BlockSpec(memory_space=pltpu.SMEM)

    def buffer(*shape, kind=F32):
        return pltpu.VMEM(shape, kind)

    scratch = [
        buffer(*embeddings.shape[::-1], kind=BF16),
        buffer(2, width, width, kind=BF16),
        buffer(2, width, width, kind=BF16),
        buffer(2, 8, 1024, kind=I32),
        buffer(4, 8, 1024, kind=I32),
        buffer(4, 8, 1024, kind=I32),
        buffer(4, rows, PAD, kind=BF16),
        buffer(4, width, PAD, kind=BF16),
        buffer(4, width, PAD, kind=BF16),
        buffer(4, rows // 2, 128),
        buffer(2, 2, width, quarter, kind=BF16),
        buffer(rows // 2, width, kind=BF16),
        buffer(4, rows // 2, PAD, kind=BF16),
        buffer(4, rows // 2, PAD, kind=BF16),
        buffer(4, 8, PAD),
        buffer(4, width, 2 * PAD, kind=BF16),
        buffer(4, width, PAD, kind=BF16),
        buffer(2, TILES, 16, 128),
        buffer(2, width, 128),
        buffer(TILES, 16, 128),
        buffer(TILES, 16, 128),
        buffer(TILES, 16, 128, kind=BF16),
        buffer(2, 3, 10, 16, 128, kind=BF16),
        buffer(2, 12, 16, 128),
        buffer(2, 4, 3, 16, 128),
        buffer(n_z, 6, 16, 128, kind=BF16),
        buffer(2, 4, 3, 16, 128, kind=BF16),
        buffer(2, 4, 10, 16, 128, kind=BF16),
        buffer(2, 4, 10, 16, 128, kind=BF16),
        buffer(2, 2, width, quarter),
        buffer(2, width, quarter),
        buffer(2, width, quarter, kind=BF16),
        buffer(2, width, quarter, kind=BF16),
        buffer(2, 2, width, quarter),
        buffer(2, width, quarter),
        buffer(width, quarter, kind=BF16),
        buffer(width, quarter, kind=BF16),
        dma((2,)),
    ]
    for shape in (
        (3,), (2,), (2,), None, (2, 3), (2, 3), (n_z - 1,),
        (2, 3), (2, 3), (2, 4), (2,), (2,), (2,), None,
    ):
        scratch += [dma if shape is None else dma(shape)] * 2
    entity, relation = pl.pallas_call(
        functools.partial(kernel, n_y, n_z, span, negs),
        out_shape=(
            jax.ShapeDtypeStruct((width, quarter), F32),
            jax.ShapeDtypeStruct(relations.shape, BF16),
        ),
        in_specs=[pl.BlockSpec(memory_space=pl.ANY)] * 2 + [vmem] * 3 + [smem] * 2,
        out_specs=(vmem, vmem),
        scratch_shapes=scratch,
        compiler_params=pltpu.CompilerParams(
            collective_id=0, has_side_effects=True, vmem_limit_bytes=56 * 2**20
        ),
    )(embeddings.T, relations, *lists[:-1], lists[-1].T)
    entity, relation = pl.pallas_call(
        hand_over,
        out_shape=(
            jax.ShapeDtypeStruct(entity.shape, F32),
            jax.ShapeDtypeStruct(relation.shape, F32),
        ),
        in_specs=[vmem] * 2,
        out_specs=(vmem, vmem),
    )(entity, relation)
    return entity.T, relation


def solution(mesh):
    n_y = 4
    n_z = mesh.shape["blk"] // (2 * n_y)
    return jax.shard_map(
        functools.partial(on_device, n_y, n_z),
        mesh=mesh,
        in_specs=(
            P("blk", None),
            P(),
            P(None, ("blk", "rep")),
            P(None, ("blk", "rep")),
            P(None, ("blk", "rep"), None),
            P(None, ("blk", "rep")),
            P(None, ("blk", "rep")),
        ),
        out_specs=(P(("blk", "rep"), None), P()),
        check_vma=False,
    )
```

```python
import functools

import jax
import jax.numpy as jnp
from jax import lax
from jax.experimental import pallas as pl
from jax.experimental.pallas import tpu as pltpu
from jax.sharding import PartitionSpec as P

MESH = pl.DeviceIdType.MESH
F32, BF16, I32 = jnp.float32, jnp.bfloat16, jnp.int32
PAD = 512
TILES = 80


def dot(a, b):
    return lax.dot_general(a, b, (((1,), (0,)), ((), ())), preferred_element_type=F32)


def dot_nt(a, b):
    return lax.dot_general(a, b, (((1,), (1,)), ((), ())), preferred_element_type=F32)


def eye(n):
    return (
        lax.broadcasted_iota(I32, (n, n), 0) == lax.broadcasted_iota(I32, (n, n), 1)
    ).astype(F32).astype(BF16)


def onehot(rows, base, index):
    shape = (rows, index.shape[1])
    return (lax.broadcasted_iota(I32, shape, 0) + base == index).astype(F32).astype(BF16)


def kernel(
    n_y, n_z, span, negs,
    emb_hbm, rel_hbm, src, tgt, neg, srel, ecnt,
    ent_out, rel_out,
    emb, rel, opt, raw, lists, sel, ohs, svt, qt, cnt, slabt, slab, oht, ngm, pgs, qhl, sgt,
    acc, acc_last, acc_in, red, red_out, r1, s1, r2, zx, g2, g1, g_other,
    tsum, tsum_in, ret, ret_in, ssum, ssum_in, half, half_in,
    load, idx_s, idx_r, slab_s, slab_r, fwd_s, fwd_r, ar0_s, ar0_r, ar1_s, ar1_r, ar2_s, ar2_r, ar3_s, ar3_r,
    ag2_s, ag2_r, ag1_s, ag1_r, ag0_s, ag0_r, tx_s, tx_r, ret_s, ret_r, sx_s, sx_r, sy_s, sy_r,
):
    width = emb.shape[0]
    n_blk = 2 * n_y * n_z
    quarter = emb.shape[1] // 4
    b, r = lax.axis_index("blk"), lax.axis_index("rep")
    xh, core = r // 2, lax.rem(r, 2)
    xl, y, z = lax.rem(b, 2), lax.rem(b // 2, n_y), b // (2 * n_y)
    x = xh * 2 + xl
    sibling = (b, xh * 2 + 1 - core)
    mate = (b, (1 - xh) * 2 + core)
    partner = (b + 1 - 2 * xl, r)

    def along_blk(k):
        return (lax.rem(b + k + n_blk, n_blk), r)

    def along_rep(k):
        return (b, lax.rem(r + k, 4))

    def x_at(k):
        return lax.rem(x + k, 4)

    def y_at(k):
        return lax.rem(y + k, n_y)

    def z_at(k):
        return lax.rem(z + k, n_z)

    def along_x(k):
        there = x_at(k)
        return ((z * n_y + y) * 2 + lax.rem(there, 2), (there // 2) * 2 + core)

    def along_y(k):
        return ((z * n_y + y_at(k)) * 2 + xl, r)

    def along_z(k):
        return ((z_at(k) * n_y + y) * 2 + xl, r)

    def send(source, target, sent, received, device):
        copy = pltpu.make_async_remote_copy(
            src_ref=source, dst_ref=target, send_sem=sent, recv_sem=received,
            device_id=device, device_id_type=MESH,
        )
        copy.start()
        return copy

    barrier = pltpu.get_barrier_semaphore()
    peers = [along_blk(k) for k in (1, 2, -1, -2)] + [along_rep(k) for k in (1, 2, 3)]
    peers += [along_x(k) for k in (1, 2, 3)] + [along_y(k) for k in range(1, n_y)]
    peers += [along_z(k) for k in range(1, n_z)]
    for peer in peers:
        pl.semaphore_signal(barrier, inc=1, device_id=peer, device_id_type=MESH)

    loads = [
        pltpu.make_async_copy(emb_hbm, emb, load.at[0]),
        pltpu.make_async_copy(rel_hbm, rel, load.at[1]),
    ]
    for copy in loads:
        copy.start()
    lane = lax.broadcasted_iota(I32, (8, 1024), 1)
    row = lax.broadcasted_iota(I32, (8, 1024), 0)
    raw[...] = jnp.zeros(raw.shape, I32)
    raw[0, 0:2, 0 : 2 * span] = src[...]
    raw[0, 2:4, 0 : 2 * span] = tgt[...]
    for s in range(2):
        raw[1, 2 * s : 2 * s + 2, 0:negs] = neg[s]
    edges = raw[0]
    second = pltpu.roll(edges, PAD - span, 1)
    edges = jnp.where(lane < PAD, edges, second)
    negatives = raw[1]
    packed = jnp.zeros((8, 1024), I32)
    for s in range(2):
        words = edges[s : s + 1] + edges[2 + s : 3 + s] * 65536
        packed = jnp.where(row == 4 * s, words, packed)
        words = negatives[2 * s : 2 * s + 1] + negatives[2 * s + 1 : 2 * s + 2] * 65536
        packed = jnp.where(row == 4 * s + 1, words, packed)
        for k in range(2):
            live = jnp.clip(ecnt[0, s] - k * span, 0, span)
            packed = jnp.where(row == 4 * s + 2 + k, srel[s, k] + live * 65536, packed)
    lists[r] = packed

    pl.semaphore_wait(barrier, len(peers))

    index_copies = [
        send(lists.at[r], lists.at[r], idx_s.at[k - 1], idx_r.at[k - 1], along_rep(k))
        for k in (2, 1, 3)
    ]
    here = pl.ds(pl.multiple_of(r * quarter, quarter), quarter)

    def send_slab(s):
        return send(
            emb_hbm.at[:, here], slabt.at[s, core], slab_s.at[s], slab_r.at[s], along_blk(s + 1)
        )

    slab_copies = {1: send_slab(1)}

    for copy in loads:
        copy.wait()
    unit = eye(width)
    for k in range(2):
        opt[k] = dot_nt(unit, rel[k]).astype(BF16)
    s1[...] = jnp.zeros(s1.shape, F32)
    for copy in index_copies:
        copy.wait()

    for s in range(2):
        before = jnp.zeros((1, 1024), I32)
        edge_words = [jnp.zeros((1, PAD), I32) for j in range(2)]
        negative_words = [jnp.zeros((1, 1024), I32) for j in range(2)]
        meta_words = [jnp.zeros((1, 1024), I32) for j in range(2)]
        for d in range(4):
            rows = lists[d]
            for k in range(2):
                meta = rows[4 * s + 2 + k : 4 * s + 3 + k]
                alive = (meta >= 65536).astype(I32)
                both = rows[4 * s + 1 : 4 * s + 2]
                negative = (both & 65535) if k == 0 else (both >> 16)
                edge = rows[4 * s : 4 * s + 1, k * PAD : (k + 1) * PAD]
                for j in range(2):
                    mine = alive * (before == 2 * core + j).astype(I32)
                    edge_words[j] += edge * mine[:, :PAD]
                    negative_words[j] += negative * mine
                    meta_words[j] += meta * mine
                before = before + alive
        lane1 = lax.broadcasted_iota(I32, (1, 1024), 1)
        for j in range(2):
            valid = lane1[:, :PAD] < (meta_words[j][:, :PAD] >> 16)
            at = 2 * s + j
            sel[at, 0:1, 0:PAD] = jnp.where(valid, edge_words[j] & 65535, -1)
            sel[at, 1:2, 0:PAD] = jnp.where(valid, edge_words[j] >> 16, -1)
            sel[at, 2:3, :] = jnp.where(lane1 < negs, negative_words[j], -1)
            sel[at, 3:4, :] = meta_words[j] & 1
            sel[at, 4:5, 0:PAD] = valid.astype(I32)

    slab_copies[1].wait_send()
    slab_copies[0] = send_slab(0)

    def operator(table, at):
        second = sel[at, 3:4, 0:width].astype(F32)
        return (
            table[0].astype(F32) * (1.0 - second) + table[1].astype(F32) * second
        ).astype(BF16)

    def queries(s):
        for j in range(2):
            at = 2 * s + j
            ohs[at] = onehot(4 * quarter, 0, sel[at, 0:1, 0:PAD])
            vectors = dot(emb[...], ohs[at]).astype(BF16)
            svt[at] = vectors
            qt[at] = dot(operator(opt, at), vectors).astype(BF16)
            times = dot(onehot(2 * quarter, 2 * xh * quarter, sel[at, 2:3, :]), jnp.ones((1024, 128), BF16))
            cnt[at] = times * (0.5 * negs**-0.5)

    def forward(s):
        slab_copies[s].wait_recv()
        return send(
            slabt.at[s, core], slabt.at[s, core], fwd_s.at[s], fwd_r.at[s], sibling
        )

    def halve(s):
        turn = eye(quarter) * jnp.asarray(0.5, BF16)
        for h in range(2):
            slab[h * quarter : (h + 1) * quarter] = dot_nt(turn, slabt[s, h]).astype(BF16)

    def score(s, js):
        turned = jnp.concatenate([slabt[s, 0], slabt[s, 1]], axis=1)
        mains, seconds = [], []
        for j in js:
            at = 2 * s + j
            oht[at] = onehot(2 * quarter, 2 * xh * quarter, sel[at, 1:2, 0:PAD])
            query = qt[at]
            target = dot(turned, oht[at])
            positive = jnp.sum(query.astype(F32) * target, axis=0, keepdims=True)
            positive_grad = -sel[at, 4:5, 0:PAD].astype(F32) * jax.nn.sigmoid(-positive)
            pgs[at, 0:1] = positive_grad
            bent = jnp.tanh(dot(slab[...], query))
            times = jnp.concatenate([cnt[at]] * (PAD // 128), axis=1)
            ngm[at] = (times * bent + times).astype(BF16)
            grad = positive_grad * target + dot(turned, ngm[at])
            high = grad.astype(BF16)
            qhl[at, :, 0:PAD] = high
            qhl[at, :, PAD:] = (grad - high.astype(F32)).astype(BF16)
            vectors = jnp.concatenate([svt[at]] * 2, axis=1)
            mains.append(dot_nt(vectors, qhl[at]))
            seconds.append(sel[at, 3:4, 0:128].astype(F32))
        return mains, seconds

    n = width // 16

    def accumulate(s, k, mains, seconds):
        first = jnp.where(k == 0, 1.0, 0.0)
        shares = [first + second * (1.0 - 2.0 * first) for second in seconds]
        for t in range(3):
            tiles = sum(
                main[:, 128 * t : 128 * t + 128] * share for main, share in zip(mains, shares)
            ).reshape(n, 16, 128)
            acc[k, n * t : n * t + n] = tiles if s == 1 else acc[k, n * t : n * t + n] + tiles
        last = sum(
            main[:, 384:width] * share[:, : width - 384] for main, share in zip(mains, shares)
        )
        last = jnp.concatenate([last, jnp.zeros((width, PAD - width), F32)], axis=1)
        if s == 1:
            acc_last[k] = last
            return
        last = acc_last[k] + last
        last = jnp.concatenate([last, jnp.zeros((PAD - width, 128), F32)], axis=0).T
        for t in range(4):
            acc[k, 3 * n + t] = last[:16, 128 * t : 128 * t + 128]
        acc[k, 3 * n + 4] = jnp.zeros((16, 128), F32)

    queries(1)
    forwards = [forward(1)]
    queries(0)
    forwards[0].wait_recv()
    halve(1)
    one = score(1, (0,))
    forwards.append(forward(0))
    two = score(1, (1,))
    for k in range(2):
        accumulate(1, k, one[0] + two[0], one[1] + two[1])
    forwards[1].wait_recv()
    halve(0)
    found = score(0, (0, 1))
    accumulate(0, 1 - core, *found)
    copy0 = send(acc.at[1 - core], acc_in, ar0_s, ar0_r, sibling)
    accumulate(0, core, *found)
    copy0.wait_recv()
    red[...] = acc[core] + acc_in[...]
    red_out[...] = red[...].astype(BF16)
    copies1 = []
    for k in (2, 1, 3):
        copies1.append(
            send(red_out.at[pl.ds(10 * x_at(k), 10)], r1.at[0, k - 1], ar1_s.at[0, k - 1], ar1_r.at[0, k - 1], along_x(k))
        )
        copies1.append(
            send(red_out.at[pl.ds(40 + 10 * y_at(k), 10)], r1.at[1, k - 1], ar1_s.at[1, k - 1], ar1_r.at[1, k - 1], along_y(k))
        )

    for s in range(2):
        positives = [(pgs[at, 0:1] * qt[at].astype(F32)).astype(BF16) for at in (2 * s, 2 * s + 1)]
        left = jnp.concatenate([qt[2 * s], qt[2 * s + 1]] + positives, axis=1)
        for h in range(2):
            rows = slice(h * quarter, (h + 1) * quarter)
            parts = [ngm[2 * s, rows], ngm[2 * s + 1, rows], oht[2 * s, rows], oht[2 * s + 1, rows]]
            tsum[s, h] = dot_nt(left, jnp.concatenate(parts, axis=1))
    tx_copies = [
        send(tsum.at[s, 1 - core], tsum_in.at[s], tx_s.at[s], tx_r.at[s], sibling)
        for s in range(2)
    ]

    for at in range(4):
        turned = operator(rel, at)
        both = jnp.concatenate([qhl[at, :, 0:PAD], qhl[at, :, PAD:]], axis=0)
        sgt[at] = dot(jnp.concatenate([turned, turned], axis=1), both).astype(BF16)

    for copy in tx_copies:
        copy.wait_recv()
    ret[0] = (tsum[0, core] + tsum_in[0]).astype(BF16)
    ret_copies = [send(ret.at[0], ret_in.at[0], ret_s.at[0], ret_r.at[0], partner)]

    for copy in copies1:
        copy.wait_recv()
    for h, at in ((0, 10 * x), (1, 40 + 10 * y)):
        total = red[pl.ds(at, 10)]
        for k in range(3):
            total += r1[h, k].astype(F32)
        s1[h, 0:10] = total
    r2[0, y] = s1[0, pl.ds(3 * y, 3)]
    r2[1, x] = s1[1, pl.ds(3 * x, 3)]
    copies2 = []
    for k in range(1, 4):
        copies2.append(
            send(s1.at[0, pl.ds(3 * y_at(k), 3)], r2.at[0, y], ar2_s.at[0, k - 1], ar2_r.at[0, k - 1], along_y(k))
        )
        copies2.append(
            send(s1.at[1, pl.ds(3 * x_at(k), 3)], r2.at[1, x], ar2_s.at[1, k - 1], ar2_r.at[1, k - 1], along_x(k))
        )

    left = jnp.concatenate([sgt[at] for at in range(4)], axis=1)
    for q in range(4):
        rows = slice(q * quarter, (q + 1) * quarter)
        ssum[q // 2, q % 2] = dot_nt(left, jnp.concatenate([ohs[at, rows] for at in range(4)], axis=1))
    sx_copies = [
        send(ssum.at[h, 1 - core], ssum_in.at[h], sx_s.at[h], sx_r.at[h], sibling)
        for h in range(2)
    ]

    for copy in copies2:
        copy.wait_recv()
    for h in range(2):
        total = (r2[h, 0] + r2[h, 1]) + (r2[h, 2] + r2[h, 3])
        zx[z, 3 * h : 3 * h + 3] = total.astype(BF16)
    copies3 = [
        send(zx.at[z], zx.at[z], ar3_s.at[k - 1], ar3_r.at[k - 1], along_z(k))
        for k in sorted(range(1, n_z), key=lambda k: -min(k, n_z - k))
    ]

    ret_copies[0].wait_recv()
    passed = ret_in[0].astype(F32) * jnp.where(xl == 1, 1.0, 0.0)
    ret[1] = (tsum[1, core] + tsum_in[1] + passed).astype(BF16)
    ret_copies.append(send(ret.at[1], ret_in.at[1], ret_s.at[1], ret_r.at[1], along_blk(-2)))
    for copy in sx_copies:
        copy.wait_recv()
    half[...] = (ssum[1 - xh, core] + ssum_in[1 - xh]).astype(BF16)
    sy_copy = send(half, half_in, sy_s, sy_r, mate)
    for copy in copies3:
        copy.wait_recv()
    total = zx[0].astype(F32)
    for k in range(1, n_z):
        total += zx[k].astype(F32)
    total = total.astype(BF16)
    g2[0, y] = total[0:3]
    g2[1, x] = total[3:6]
    copies = []
    for k in (2, 1, 3):
        copies.append(send(g2.at[0, y], g2.at[0, y], ag2_s.at[0, k - 1], ag2_r.at[0, k - 1], along_y(k)))
        copies.append(send(g2.at[1, x], g2.at[1, x], ag2_s.at[1, k - 1], ag2_r.at[1, k - 1], along_x(k)))
    sends = list(copies)
    for copy in copies:
        copy.wait_recv()
    for h, at in ((0, x), (1, y)):
        for k in range(3):
            g1[h, at, 3 * k : 3 * k + 3] = g2[h, k]
        g1[h, at, 9] = g2[h, 3, 0]
    copies = []
    for k in (2, 1, 3):
        copies.append(send(g1.at[0, x], g1.at[0, x], ag1_s.at[0, k - 1], ag1_r.at[0, k - 1], along_x(k)))
        copies.append(send(g1.at[1, y], g1.at[1, y], ag1_s.at[1, k - 1], ag1_r.at[1, k - 1], along_y(k)))
    sends += copies
    handed = [
        send(g1.at[h, at], g_other.at[h, at], ag0_s.at[h, 0], ag0_r.at[h, 0], sibling)
        for h, at in ((0, x), (1, y))
    ]

    sy_copy.wait_recv()
    ret_copies[1].wait_recv()
    total = (ssum[xh, core] + ssum_in[xh]) + half_in[...].astype(F32)
    mine = ret_in[0].astype(F32) * jnp.where(xl == 0, 1.0, 0.0)
    total = total + (mine + ret_in[1].astype(F32))
    ent_out[...] = total

    for i, k in ((1, 1), (2, 3), (0, 2)):
        copies[2 * i].wait_recv()
        copies[2 * i + 1].wait_recv()
        for h, at in ((0, x_at(4 - k)), (1, y_at(4 - k))):
            handed.append(
                send(g1.at[h, at], g_other.at[h, at], ag0_s.at[h, k], ag0_r.at[h, k], sibling)
            )

    def write(k, tiles):
        for t in range(3):
            rel_out[k, :, 128 * t : 128 * t + 128] = tiles[n * t : n * t + n].reshape(width, 128)
        rest = jnp.concatenate([tiles[3 * n + t].astype(F32) for t in range(4)], axis=1)
        rest = jnp.concatenate([rest, jnp.zeros((112, PAD), F32)], axis=0)
        rel_out[k, :, 384:width] = rest.T[:width, : width - 384].astype(BF16)

    write(core, g1[...].reshape(TILES, 16, 128))
    for copy in handed:
        copy.wait_recv()
    write(1 - core, g_other[...].reshape(TILES, 16, 128))

    for copy in [slab_copies[0]] + forwards + [copy0, sy_copy] + handed + sends:
        copy.wait_send()
    for copy in tx_copies + copies1 + copies2 + copies3 + sx_copies + ret_copies:
        copy.wait_send()


def hand_over(entity, relation, entity_out, relation_out):
    entity_out[...] = entity[...]
    relation_out[...] = relation[...].astype(F32)


def on_device(n_y, n_z, embeddings, relations, *lists):
    rows, width = embeddings.shape
    quarter = rows // 4
    span = lists[0].shape[1] // 2
    negs = lists[2].shape[2]
    dma = pltpu.SemaphoreType.DMA
    vmem, smem = pl.BlockSpec(memory_space=pltpu.VMEM), pl.BlockSpec(memory_space=pltpu.SMEM)

    def buffer(*shape, kind=F32):
        return pltpu.VMEM(shape, kind)

    scratch = [
        buffer(*embeddings.shape[::-1], kind=BF16),
        buffer(2, width, width, kind=BF16),
        buffer(2, width, width, kind=BF16),
        buffer(2, 8, 1024, kind=I32),
        buffer(4, 8, 1024, kind=I32),
        buffer(4, 8, 1024, kind=I32),
        buffer(4, rows, PAD, kind=BF16),
        buffer(4, width, PAD, kind=BF16),
        buffer(4, width, PAD, kind=BF16),
        buffer(4, rows // 2, 128),
        buffer(2, 2, width, quarter, kind=BF16),
        buffer(rows // 2, width, kind=BF16),
        buffer(4, rows // 2, PAD, kind=BF16),
        buffer(4, rows // 2, PAD, kind=BF16),
        buffer(4, 8, PAD),
        buffer(4, width, 2 * PAD, kind=BF16),
        buffer(4, width, PAD, kind=BF16),
        buffer(2, TILES, 16, 128),
        buffer(2, width, 128),
        buffer(TILES, 16, 128),
        buffer(TILES, 16, 128),
        buffer(TILES, 16, 128, kind=BF16),
        buffer(2, 3, 10, 16, 128, kind=BF16),
        buffer(2, 12, 16, 128),
        buffer(2, 4, 3, 16, 128),
        buffer(n_z, 6, 16, 128, kind=BF16),
        buffer(2, 4, 3, 16, 128, kind=BF16),
        buffer(2, 4, 10, 16, 128, kind=BF16),
        buffer(2, 4, 10, 16, 128, kind=BF16),
        buffer(2, 2, width, quarter),
        buffer(2, width, quarter),
        buffer(2, width, quarter, kind=BF16),
        buffer(2, width, quarter, kind=BF16),
        buffer(2, 2, width, quarter),
        buffer(2, width, quarter),
        buffer(width, quarter, kind=BF16),
        buffer(width, quarter, kind=BF16),
        dma((2,)),
    ]
    for shape in (
        (3,), (2,), (2,), None, (2, 3), (2, 3), (n_z - 1,),
        (2, 3), (2, 3), (2, 4), (2,), (2,), (2,), None,
    ):
        scratch += [dma if shape is None else dma(shape)] * 2
    entity, relation = pl.pallas_call(
        functools.partial(kernel, n_y, n_z, span, negs),
        out_shape=(
            jax.ShapeDtypeStruct((width, quarter), F32),
            jax.ShapeDtypeStruct(relations.shape, BF16),
        ),
        in_specs=[pl.BlockSpec(memory_space=pl.ANY)] * 2 + [vmem] * 3 + [smem] * 2,
        out_specs=(vmem, vmem),
        scratch_shapes=scratch,
        compiler_params=pltpu.CompilerParams(
            collective_id=0, has_side_effects=True, vmem_limit_bytes=56 * 2**20
        ),
    )(embeddings.T, relations, *lists[:-1], lists[-1].T)
    entity, relation = pl.pallas_call(
        hand_over,
        out_shape=(
            jax.ShapeDtypeStruct(entity.shape, F32),
            jax.ShapeDtypeStruct(relation.shape, F32),
        ),
        in_specs=[vmem] * 2,
        out_specs=(vmem, vmem),
    )(entity, relation)
    return entity.T, relation


def solution(mesh):
    n_y = 4
    n_z = mesh.shape["blk"] // (2 * n_y)
    return jax.shard_map(
        functools.partial(on_device, n_y, n_z),
        mesh=mesh,
        in_specs=(
            P("blk", None),
            P(),
            P(None, ("blk", "rep")),
            P(None, ("blk", "rep")),
            P(None, ("blk", "rep"), None),
            P(None, ("blk", "rep")),
            P(None, ("blk", "rep")),
        ),
        out_specs=(P(("blk", "rep"), None), P()),
        check_vma=False,
    )
```

```python
import functools

import jax
import jax.numpy as jnp
from jax import lax
from jax.experimental import pallas as pl
from jax.experimental.pallas import tpu as pltpu
from jax.sharding import PartitionSpec as P

MESH = pl.DeviceIdType.MESH
F32, BF16, I32 = jnp.float32, jnp.bfloat16, jnp.int32
PAD = 512
TILES = 80


def dot(a, b):
    return lax.dot_general(a, b, (((1,), (0,)), ((), ())), preferred_element_type=F32)


def dot_nt(a, b):
    return lax.dot_general(a, b, (((1,), (1,)), ((), ())), preferred_element_type=F32)


def eye(n):
    return (
        lax.broadcasted_iota(I32, (n, n), 0) == lax.broadcasted_iota(I32, (n, n), 1)
    ).astype(F32).astype(BF16)


def onehot(rows, base, index):
    shape = (rows, index.shape[1])
    return (lax.broadcasted_iota(I32, shape, 0) + base == index).astype(F32).astype(BF16)


def kernel(
    n_y, n_z, span, negs,
    emb_hbm, rel_hbm, src, tgt, neg, srel, ecnt,
    ent_out, rel_out,
    emb, rel, opt, raw, lists, sel, ohs, svt, qt, cnt, slabt, slab, oht, ngm, pgs, qhl, sgt,
    acc, acc_last, acc_in, red, red_out, r1, s1, r2, zx, g2, g1, g_other,
    tsum, tsum_in, ret, ret_in, ssum, ssum_in, half, half_in,
    load, idx_s, idx_r, slab_s, slab_r, fwd_s, fwd_r, ar0_s, ar0_r, ar1_s, ar1_r, ar2_s, ar2_r, ar3_s, ar3_r,
    ag2_s, ag2_r, ag1_s, ag1_r, ag0_s, ag0_r, tx_s, tx_r, ret_s, ret_r, sx_s, sx_r, sy_s, sy_r,
):
    width = emb.shape[0]
    n_blk = 2 * n_y * n_z
    quarter = emb.shape[1] // 4
    b, r = lax.axis_index("blk"), lax.axis_index("rep")
    xh, core = r // 2, lax.rem(r, 2)
    xl, y, z = lax.rem(b, 2), lax.rem(b // 2, n_y), b // (2 * n_y)
    x = xh * 2 + xl
    sibling = (b, xh * 2 + 1 - core)
    mate = (b, (1 - xh) * 2 + core)
    partner = (b + 1 - 2 * xl, r)

    def along_blk(k):
        return (lax.rem(b + k + n_blk, n_blk), r)

    def along_rep(k):
        return (b, lax.rem(r + k, 4))

    def x_at(k):
        return lax.rem(x + k, 4)

    def y_at(k):
        return lax.rem(y + k, n_y)

    def z_at(k):
        return lax.rem(z + k, n_z)

    def along_x(k):
        there = x_at(k)
        return ((z * n_y + y) * 2 + lax.rem(there, 2), (there // 2) * 2 + core)

    def along_y(k):
        return ((z * n_y + y_at(k)) * 2 + xl, r)

    def along_z(k):
        return ((z_at(k) * n_y + y) * 2 + xl, r)

    def send(source, target, sent, received, device):
        copy = pltpu.make_async_remote_copy(
            src_ref=source, dst_ref=target, send_sem=sent, recv_sem=received,
            device_id=device, device_id_type=MESH,
        )
        copy.start()
        return copy

    barrier = pltpu.get_barrier_semaphore()
    peers = [along_blk(k) for k in (1, 2, -1, -2)] + [along_rep(k) for k in (1, 2, 3)]
    peers += [along_x(k) for k in (1, 2, 3)] + [along_y(k) for k in range(1, n_y)]
    peers += [along_z(k) for k in range(1, n_z)]
    for peer in peers:
        pl.semaphore_signal(barrier, inc=1, device_id=peer, device_id_type=MESH)

    loads = [
        pltpu.make_async_copy(emb_hbm, emb, load.at[0]),
        pltpu.make_async_copy(rel_hbm, rel, load.at[1]),
    ]
    for copy in loads:
        copy.start()
    lane = lax.broadcasted_iota(I32, (8, 1024), 1)
    row = lax.broadcasted_iota(I32, (8, 1024), 0)
    raw[...] = jnp.zeros(raw.shape, I32)
    raw[0, 0:2, 0 : 2 * span] = src[...]
    raw[0, 2:4, 0 : 2 * span] = tgt[...]
    for s in range(2):
        raw[1, 2 * s : 2 * s + 2, 0:negs] = neg[s]
    edges = raw[0]
    second = pltpu.roll(edges, PAD - span, 1)
    edges = jnp.where(lane < PAD, edges, second)
    negatives = raw[1]
    packed = jnp.zeros((8, 1024), I32)
    for s in range(2):
        words = edges[s : s + 1] + edges[2 + s : 3 + s] * 65536
        packed = jnp.where(row == 4 * s, words, packed)
        words = negatives[2 * s : 2 * s + 1] + negatives[2 * s + 1 : 2 * s + 2] * 65536
        packed = jnp.where(row == 4 * s + 1, words, packed)
        for k in range(2):
            live = jnp.clip(ecnt[0, s] - k * span, 0, span)
            packed = jnp.where(row == 4 * s + 2 + k, srel[s, k] + live * 65536, packed)
    lists[r] = packed

    pl.semaphore_wait(barrier, len(peers))

    index_copies = [
        send(lists.at[r], lists.at[r], idx_s.at[k - 1], idx_r.at[k - 1], along_rep(k))
        for k in (2, 1, 3)
    ]
    here = pl.ds(pl.multiple_of(r * quarter, quarter), quarter)

    def send_slab(s):
        return send(
            emb_hbm.at[:, here], slabt.at[s, core], slab_s.at[s], slab_r.at[s], along_blk(s + 1)
        )

    slab_copies = {1: send_slab(1)}

    for copy in loads:
        copy.wait()
    unit = eye(width)
    for k in range(2):
        opt[k] = dot_nt(unit, rel[k]).astype(BF16)
    s1[...] = jnp.zeros(s1.shape, F32)
    for copy in index_copies:
        copy.wait()

    for s in range(2):
        before = jnp.zeros((1, 1024), I32)
        edge_words = [jnp.zeros((1, PAD), I32) for j in range(2)]
        negative_words = [jnp.zeros((1, 1024), I32) for j in range(2)]
        meta_words = [jnp.zeros((1, 1024), I32) for j in range(2)]
        for d in range(4):
            rows = lists[d]
            for k in range(2):
                meta = rows[4 * s + 2 + k : 4 * s + 3 + k]
                alive = (meta >= 65536).astype(I32)
                both = rows[4 * s + 1 : 4 * s + 2]
                negative = (both & 65535) if k == 0 else (both >> 16)
                edge = rows[4 * s : 4 * s + 1, k * PAD : (k + 1) * PAD]
                for j in range(2):
                    mine = alive * (before == 2 * core + j).astype(I32)
                    edge_words[j] += edge * mine[:, :PAD]
                    negative_words[j] += negative * mine
                    meta_words[j] += meta * mine
                before = before + alive
        lane1 = lax.broadcasted_iota(I32, (1, 1024), 1)
        for j in range(2):
            valid = lane1[:, :PAD] < (meta_words[j][:, :PAD] >> 16)
            at = 2 * s + j
            sel[at, 0:1, 0:PAD] = jnp.where(valid, edge_words[j] & 65535, -1)
            sel[at, 1:2, 0:PAD] = jnp.where(valid, edge_words[j] >> 16, -1)
            sel[at, 2:3, :] = jnp.where(lane1 < negs, negative_words[j], -1)
            sel[at, 3:4, :] = meta_words[j] & 1
            sel[at, 4:5, 0:PAD] = valid.astype(I32)

    slab_copies[1].wait_send()
    slab_copies[0] = send_slab(0)

    def operator(table, at):
        second = sel[at, 3:4, 0:width].astype(F32)
        return (
            table[0].astype(F32) * (1.0 - second) + table[1].astype(F32) * second
        ).astype(BF16)

    def queries(s):
        for j in range(2):
            at = 2 * s + j
            ohs[at] = onehot(4 * quarter, 0, sel[at, 0:1, 0:PAD])
            vectors = dot(emb[...], ohs[at]).astype(BF16)
            svt[at] = vectors
            qt[at] = dot(operator(opt, at), vectors).astype(BF16)
            times = dot(onehot(2 * quarter, 2 * xh * quarter, sel[at, 2:3, :]), jnp.ones((1024, 128), BF16))
            cnt[at] = times * (0.5 * negs**-0.5)

    def forward(s):
        slab_copies[s].wait_recv()
        return send(
            slabt.at[s, core], slabt.at[s, core], fwd_s.at[s], fwd_r.at[s], sibling
        )

    def halve(s):
        turn = eye(quarter) * jnp.asarray(0.5, BF16)
        for h in range(2):
            slab[h * quarter : (h + 1) * quarter] = dot_nt(turn, slabt[s, h]).astype(BF16)

    def score(s, js):
        turned = jnp.concatenate([slabt[s, 0], slabt[s, 1]], axis=1)
        mains, seconds = [], []
        for j in js:
            at = 2 * s + j
            oht[at] = onehot(2 * quarter, 2 * xh * quarter, sel[at, 1:2, 0:PAD])
            query = qt[at]
            target = dot(turned, oht[at])
            positive = jnp.sum(query.astype(F32) * target, axis=0, keepdims=True)
            positive_grad = -sel[at, 4:5, 0:PAD].astype(F32) * jax.nn.sigmoid(-positive)
            pgs[at, 0:1] = positive_grad
            bent = jnp.tanh(dot(slab[...], query))
            times = jnp.concatenate([cnt[at]] * (PAD // 128), axis=1)
            ngm[at] = (times * bent + times).astype(BF16)
            grad = positive_grad * target + dot(turned, ngm[at])
            high = grad.astype(BF16)
            qhl[at, :, 0:PAD] = high
            qhl[at, :, PAD:] = (grad - high.astype(F32)).astype(BF16)
            mains.append(dot_nt(svt[at], high))
            seconds.append(sel[at, 3:4, 0:128].astype(F32))
        return mains, seconds

    n = width // 16

    def accumulate(s, k, mains, seconds):
        first = jnp.where(k == 0, 1.0, 0.0)
        shares = [first + second * (1.0 - 2.0 * first) for second in seconds]
        for t in range(3):
            tiles = sum(
                main[:, 128 * t : 128 * t + 128] * share for main, share in zip(mains, shares)
            ).reshape(n, 16, 128)
            acc[k, n * t : n * t + n] = tiles if s == 1 else acc[k, n * t : n * t + n] + tiles
        last = sum(
            main[:, 384:width] * share[:, : width - 384] for main, share in zip(mains, shares)
        )
        last = jnp.concatenate([last, jnp.zeros((width, PAD - width), F32)], axis=1)
        if s == 1:
            acc_last[k] = last
            return
        last = acc_last[k] + last
        last = jnp.concatenate([last, jnp.zeros((PAD - width, 128), F32)], axis=0).T
        for t in range(4):
            acc[k, 3 * n + t] = last[:16, 128 * t : 128 * t + 128]
        acc[k, 3 * n + 4] = jnp.zeros((16, 128), F32)

    queries(1)
    forwards = [forward(1)]
    queries(0)
    forwards[0].wait_recv()
    halve(1)
    one = score(1, (0,))
    forwards.append(forward(0))
    two = score(1, (1,))
    for k in range(2):
        accumulate(1, k, one[0] + two[0], one[1] + two[1])
    forwards[1].wait_recv()
    halve(0)
    found = score(0, (0, 1))
    accumulate(0, 1 - core, *found)
    copy0 = send(acc.at[1 - core], acc_in, ar0_s, ar0_r, sibling)
    accumulate(0, core, *found)
    copy0.wait_recv()
    red[...] = acc[core] + acc_in[...]
    red_out[...] = red[...].astype(BF16)
    copies1 = []
    for k in (2, 1, 3):
        copies1.append(
            send(red_out.at[pl.ds(10 * x_at(k), 10)], r1.at[0, k - 1], ar1_s.at[0, k - 1], ar1_r.at[0, k - 1], along_x(k))
        )
        copies1.append(
            send(red_out.at[pl.ds(40 + 10 * y_at(k), 10)], r1.at[1, k - 1], ar1_s.at[1, k - 1], ar1_r.at[1, k - 1], along_y(k))
        )

    for s in range(2):
        positives = [(pgs[at, 0:1] * qt[at].astype(F32)).astype(BF16) for at in (2 * s, 2 * s + 1)]
        left = jnp.concatenate([qt[2 * s], qt[2 * s + 1]] + positives, axis=1)
        for h in range(2):
            rows = slice(h * quarter, (h + 1) * quarter)
            parts = [ngm[2 * s, rows], ngm[2 * s + 1, rows], oht[2 * s, rows], oht[2 * s + 1, rows]]
            tsum[s, h] = dot_nt(left, jnp.concatenate(parts, axis=1))
    tx_copies = [
        send(tsum.at[s, 1 - core], tsum_in.at[s], tx_s.at[s], tx_r.at[s], sibling)
        for s in range(2)
    ]

    for at in range(4):
        turned = operator(rel, at)
        both = jnp.concatenate([qhl[at, :, 0:PAD], qhl[at, :, PAD:]], axis=0)
        sgt[at] = dot(jnp.concatenate([turned, turned], axis=1), both).astype(BF16)

    for copy in copies1:
        copy.wait_recv()
    for h, at in ((0, 10 * x), (1, 40 + 10 * y)):
        total = red[pl.ds(at, 10)]
        for k in range(3):
            total += r1[h, k].astype(F32)
        s1[h, 0:10] = total
    r2[0, y] = s1[0, pl.ds(3 * y, 3)]
    r2[1, x] = s1[1, pl.ds(3 * x, 3)]
    copies2 = []
    for k in (2, 1, 3):
        copies2.append(
            send(s1.at[0, pl.ds(3 * y_at(k), 3)], r2.at[0, y], ar2_s.at[0, k - 1], ar2_r.at[0, k - 1], along_y(k))
        )
        copies2.append(
            send(s1.at[1, pl.ds(3 * x_at(k), 3)], r2.at[1, x], ar2_s.at[1, k - 1], ar2_r.at[1, k - 1], along_x(k))
        )

    for copy in tx_copies:
        copy.wait_recv()
    ret[0] = (tsum[0, core] + tsum_in[0]).astype(BF16)
    ret_copies = [send(ret.at[0], ret_in.at[0], ret_s.at[0], ret_r.at[0], partner)]

    left = jnp.concatenate([sgt[at] for at in range(4)], axis=1)
    for q in range(4):
        rows = slice(q * quarter, (q + 1) * quarter)
        ssum[q // 2, q % 2] = dot_nt(left, jnp.concatenate([ohs[at, rows] for at in range(4)], axis=1))
    sx_copies = [
        send(ssum.at[h, 1 - core], ssum_in.at[h], sx_s.at[h], sx_r.at[h], sibling)
        for h in range(2)
    ]

    for copy in copies2:
        copy.wait_recv()
    for h in range(2):
        total = (r2[h, 0] + r2[h, 1]) + (r2[h, 2] + r2[h, 3])
        zx[z, 3 * h : 3 * h + 3] = total.astype(BF16)
    copies3 = [
        send(zx.at[z], zx.at[z], ar3_s.at[k - 1], ar3_r.at[k - 1], along_z(k))
        for k in sorted(range(1, n_z), key=lambda k: -min(k, n_z - k))
    ]

    for copy in sx_copies:
        copy.wait_recv()
    half[...] = (ssum[1 - xh, core] + ssum_in[1 - xh]).astype(BF16)
    sy_copy = send(half, half_in, sy_s, sy_r, mate)
    ret_copies[0].wait_recv()
    passed = ret_in[0].astype(F32) * jnp.where(xl == 1, 1.0, 0.0)
    ret[1] = (tsum[1, core] + tsum_in[1] + passed).astype(BF16)
    ret_copies.append(send(ret.at[1], ret_in.at[1], ret_s.at[1], ret_r.at[1], along_blk(-2)))
    for copy in copies3:
        copy.wait_recv()
    total = zx[0].astype(F32)
    for k in range(1, n_z):
        total += zx[k].astype(F32)
    total = total.astype(BF16)
    g2[0, y] = total[0:3]
    g2[1, x] = total[3:6]
    copies = []
    for k in (2, 1, 3):
        copies.append(send(g2.at[0, y], g2.at[0, y], ag2_s.at[0, k - 1], ag2_r.at[0, k - 1], along_y(k)))
        copies.append(send(g2.at[1, x], g2.at[1, x], ag2_s.at[1, k - 1], ag2_r.at[1, k - 1], along_x(k)))
    sends = list(copies)
    for copy in copies:
        copy.wait_recv()
    for h, at in ((0, x), (1, y)):
        for k in range(3):
            g1[h, at, 3 * k : 3 * k + 3] = g2[h, k]
        g1[h, at, 9] = g2[h, 3, 0]
    copies = []
    for k in (2, 1, 3):
        copies.append(send(g1.at[0, x], g1.at[0, x], ag1_s.at[0, k - 1], ag1_r.at[0, k - 1], along_x(k)))
        copies.append(send(g1.at[1, y], g1.at[1, y], ag1_s.at[1, k - 1], ag1_r.at[1, k - 1], along_y(k)))
    sends += copies
    handed = [
        send(g1.at[h, at], g_other.at[h, at], ag0_s.at[h, 0], ag0_r.at[h, 0], sibling)
        for h, at in ((0, x), (1, y))
    ]

    sy_copy.wait_recv()
    ret_copies[1].wait_recv()
    total = (ssum[xh, core] + ssum_in[xh]) + half_in[...].astype(F32)
    mine = ret_in[0].astype(F32) * jnp.where(xl == 0, 1.0, 0.0)
    total = total + (mine + ret_in[1].astype(F32))
    ent_out[...] = total

    for i, k in ((1, 1), (2, 3), (0, 2)):
        copies[2 * i].wait_recv()
        copies[2 * i + 1].wait_recv()
        for h, at in ((0, x_at(4 - k)), (1, y_at(4 - k))):
            handed.append(
                send(g1.at[h, at], g_other.at[h, at], ag0_s.at[h, k], ag0_r.at[h, k], sibling)
            )

    def write(k, tiles):
        for t in range(3):
            rel_out[k, :, 128 * t : 128 * t + 128] = tiles[n * t : n * t + n].reshape(width, 128)
        rest = jnp.concatenate([tiles[3 * n + t].astype(F32) for t in range(4)], axis=1)
        rest = jnp.concatenate([rest, jnp.zeros((112, PAD), F32)], axis=0)
        rel_out[k, :, 384:width] = rest.T[:width, : width - 384].astype(BF16)

    write(core, g1[...].reshape(TILES, 16, 128))
    for copy in handed:
        copy.wait_recv()
    write(1 - core, g_other[...].reshape(TILES, 16, 128))

    for copy in [slab_copies[0]] + forwards + [copy0, sy_copy] + handed + sends:
        copy.wait_send()
    for copy in tx_copies + copies1 + copies2 + copies3 + sx_copies + ret_copies:
        copy.wait_send()


def hand_over(entity, relation, entity_out, relation_out):
    entity_out[...] = entity[...]
    relation_out[...] = relation[...].astype(F32)


def on_device(n_y, n_z, embeddings, relations, *lists):
    rows, width = embeddings.shape
    quarter = rows // 4
    span = lists[0].shape[1] // 2
    negs = lists[2].shape[2]
    dma = pltpu.SemaphoreType.DMA
    vmem, smem = pl.BlockSpec(memory_space=pltpu.VMEM), pl.BlockSpec(memory_space=pltpu.SMEM)

    def buffer(*shape, kind=F32):
        return pltpu.VMEM(shape, kind)

    scratch = [
        buffer(*embeddings.shape[::-1], kind=BF16),
        buffer(2, width, width, kind=BF16),
        buffer(2, width, width, kind=BF16),
        buffer(2, 8, 1024, kind=I32),
        buffer(4, 8, 1024, kind=I32),
        buffer(4, 8, 1024, kind=I32),
        buffer(4, rows, PAD, kind=BF16),
        buffer(4, width, PAD, kind=BF16),
        buffer(4, width, PAD, kind=BF16),
        buffer(4, rows // 2, 128),
        buffer(2, 2, width, quarter, kind=BF16),
        buffer(rows // 2, width, kind=BF16),
        buffer(4, rows // 2, PAD, kind=BF16),
        buffer(4, rows // 2, PAD, kind=BF16),
        buffer(4, 8, PAD),
        buffer(4, width, 2 * PAD, kind=BF16),
        buffer(4, width, PAD, kind=BF16),
        buffer(2, TILES, 16, 128),
        buffer(2, width, 128),
        buffer(TILES, 16, 128),
        buffer(TILES, 16, 128),
        buffer(TILES, 16, 128, kind=BF16),
        buffer(2, 3, 10, 16, 128, kind=BF16),
        buffer(2, 12, 16, 128),
        buffer(2, 4, 3, 16, 128),
        buffer(n_z, 6, 16, 128, kind=BF16),
        buffer(2, 4, 3, 16, 128, kind=BF16),
        buffer(2, 4, 10, 16, 128, kind=BF16),
        buffer(2, 4, 10, 16, 128, kind=BF16),
        buffer(2, 2, width, quarter),
        buffer(2, width, quarter),
        buffer(2, width, quarter, kind=BF16),
        buffer(2, width, quarter, kind=BF16),
        buffer(2, 2, width, quarter),
        buffer(2, width, quarter),
        buffer(width, quarter, kind=BF16),
        buffer(width, quarter, kind=BF16),
        dma((2,)),
    ]
    for shape in (
        (3,), (2,), (2,), None, (2, 3), (2, 3), (n_z - 1,),
        (2, 3), (2, 3), (2, 4), (2,), (2,), (2,), None,
    ):
        scratch += [dma if shape is None else dma(shape)] * 2
    entity, relation = pl.pallas_call(
        functools.partial(kernel, n_y, n_z, span, negs),
        out_shape=(
            jax.ShapeDtypeStruct((width, quarter), F32),
            jax.ShapeDtypeStruct(relations.shape, BF16),
        ),
        in_specs=[pl.BlockSpec(memory_space=pl.ANY)] * 2 + [vmem] * 3 + [smem] * 2,
        out_specs=(vmem, vmem),
        scratch_shapes=scratch,
        compiler_params=pltpu.CompilerParams(
            collective_id=0, has_side_effects=True, vmem_limit_bytes=56 * 2**20
        ),
    )(embeddings.T, relations, *lists[:-1], lists[-1].T)
    blocks = [
        pl.BlockSpec((width // 2, quarter), lambda i: (i, 0)),
        pl.BlockSpec((1, width, width), lambda i: (i, 0, 0)),
    ]
    entity, relation = pl.pallas_call(
        hand_over,
        out_shape=(
            jax.ShapeDtypeStruct(entity.shape, F32),
            jax.ShapeDtypeStruct(relation.shape, F32),
        ),
        grid=(2,),
        in_specs=blocks,
        out_specs=tuple(blocks),
    )(entity, relation)
    return entity.T, relation


def solution(mesh):
    n_y = 4
    n_z = mesh.shape["blk"] // (2 * n_y)
    return jax.shard_map(
        functools.partial(on_device, n_y, n_z),
        mesh=mesh,
        in_specs=(
            P("blk", None),
            P(),
            P(None, ("blk", "rep")),
            P(None, ("blk", "rep")),
            P(None, ("blk", "rep"), None),
            P(None, ("blk", "rep")),
            P(None, ("blk", "rep")),
        ),
        out_specs=(P(("blk", "rep"), None), P()),
        check_vma=False,
    )
```

```python
import functools

import jax
import jax.numpy as jnp
from jax import lax
from jax.experimental import pallas as pl
from jax.experimental.pallas import tpu as pltpu
from jax.sharding import PartitionSpec as P

MESH = pl.DeviceIdType.MESH
F32, BF16, I32 = jnp.float32, jnp.bfloat16, jnp.int32
PAD = 512
TILES = 80


def dot(a, b):
    return lax.dot_general(a, b, (((1,), (0,)), ((), ())), preferred_element_type=F32)


def dot_nt(a, b):
    return lax.dot_general(a, b, (((1,), (1,)), ((), ())), preferred_element_type=F32)


def eye(n):
    return (
        lax.broadcasted_iota(I32, (n, n), 0) == lax.broadcasted_iota(I32, (n, n), 1)
    ).astype(F32).astype(BF16)


def onehot(rows, base, index):
    shape = (rows, index.shape[1])
    return (lax.broadcasted_iota(I32, shape, 0) + base == index).astype(F32).astype(BF16)


def kernel(
    n_y, n_z, span, negs,
    emb_hbm, rel_hbm, src, tgt, neg, srel, ecnt,
    ent_out, rel_out,
    emb, rel, opt, raw, lists, sel, ohs, svt, qt, cnt, slabt, slab, oht, ngm, pgs, qhl, sgt,
    acc, acc_last, acc_out, acc_in, red, red_out, r1, s1, r2, zx, g2, g1, g_other,
    tsum, tsum_in, ret, ret_in, ssum, ssum_in, half, half_in,
    load, idx_s, idx_r, slab_s, slab_r, fwd_s, fwd_r, ar0_s, ar0_r, ar1_s, ar1_r, ar2_s, ar2_r, ar3_s, ar3_r,
    ag2_s, ag2_r, ag1_s, ag1_r, ag0_s, ag0_r, tx_s, tx_r, ret_s, ret_r, sx_s, sx_r, sy_s, sy_r,
):
    width = emb.shape[0]
    n_blk = 2 * n_y * n_z
    quarter = emb.shape[1] // 4
    b, r = lax.axis_index("blk"), lax.axis_index("rep")
    xh, core = r // 2, lax.rem(r, 2)
    xl, y, z = lax.rem(b, 2), lax.rem(b // 2, n_y), b // (2 * n_y)
    x = xh * 2 + xl
    sibling = (b, xh * 2 + 1 - core)
    mate = (b, (1 - xh) * 2 + core)
    partner = (b + 1 - 2 * xl, r)

    def along_blk(k):
        return (lax.rem(b + k + n_blk, n_blk), r)

    def along_rep(k):
        return (b, lax.rem(r + k, 4))

    def x_at(k):
        return lax.rem(x + k, 4)

    def y_at(k):
        return lax.rem(y + k, n_y)

    def z_at(k):
        return lax.rem(z + k, n_z)

    def along_x(k):
        there = x_at(k)
        return ((z * n_y + y) * 2 + lax.rem(there, 2), (there // 2) * 2 + core)

    def along_y(k):
        return ((z * n_y + y_at(k)) * 2 + xl, r)

    def along_z(k):
        return ((z_at(k) * n_y + y) * 2 + xl, r)

    def send(source, target, sent, received, device):
        copy = pltpu.make_async_remote_copy(
            src_ref=source, dst_ref=target, send_sem=sent, recv_sem=received,
            device_id=device, device_id_type=MESH,
        )
        copy.start()
        return copy

    barrier = pltpu.get_barrier_semaphore()
    peers = [along_blk(k) for k in (1, 2, -1, -2)] + [along_rep(k) for k in (1, 2, 3)]
    peers += [along_x(k) for k in (1, 2, 3)] + [along_y(k) for k in range(1, n_y)]
    peers += [along_z(k) for k in range(1, n_z)]
    for peer in peers:
        pl.semaphore_signal(barrier, inc=1, device_id=peer, device_id_type=MESH)

    loads = [
        pltpu.make_async_copy(emb_hbm, emb, load.at[0]),
        pltpu.make_async_copy(rel_hbm, rel, load.at[1]),
    ]
    for copy in loads:
        copy.start()
    lane = lax.broadcasted_iota(I32, (8, 1024), 1)
    row = lax.broadcasted_iota(I32, (8, 1024), 0)
    raw[...] = jnp.zeros(raw.shape, I32)
    raw[0, 0:2, 0 : 2 * span] = src[...]
    raw[0, 2:4, 0 : 2 * span] = tgt[...]
    for s in range(2):
        raw[1, 2 * s : 2 * s + 2, 0:negs] = neg[s]
    edges = raw[0]
    second = pltpu.roll(edges, PAD - span, 1)
    edges = jnp.where(lane < PAD, edges, second)
    negatives = raw[1]
    packed = jnp.zeros((8, 1024), I32)
    for s in range(2):
        words = edges[s : s + 1] + edges[2 + s : 3 + s] * 65536
        packed = jnp.where(row == 4 * s, words, packed)
        words = negatives[2 * s : 2 * s + 1] + negatives[2 * s + 1 : 2 * s + 2] * 65536
        packed = jnp.where(row == 4 * s + 1, words, packed)
        for k in range(2):
            live = jnp.clip(ecnt[0, s] - k * span, 0, span)
            packed = jnp.where(row == 4 * s + 2 + k, srel[s, k] + live * 65536, packed)
    lists[r] = packed

    pl.semaphore_wait(barrier, len(peers))

    index_copies = [
        send(lists.at[r], lists.at[r], idx_s.at[k - 1], idx_r.at[k - 1], along_rep(k))
        for k in (2, 1, 3)
    ]
    here = pl.ds(pl.multiple_of(r * quarter, quarter), quarter)

    def send_slab(s):
        return send(
            emb_hbm.at[:, here], slabt.at[s, core], slab_s.at[s], slab_r.at[s], along_blk(s + 1)
        )

    slab_copies = {1: send_slab(1)}

    for copy in loads:
        copy.wait()
    unit = eye(width)
    for k in range(2):
        opt[k] = dot_nt(unit, rel[k]).astype(BF16)
    s1[...] = jnp.zeros(s1.shape, F32)
    for copy in index_copies:
        copy.wait()

    for s in range(2):
        before = jnp.zeros((1, 1024), I32)
        edge_words = [jnp.zeros((1, PAD), I32) for j in range(2)]
        negative_words = [jnp.zeros((1, 1024), I32) for j in range(2)]
        meta_words = [jnp.zeros((1, 1024), I32) for j in range(2)]
        for d in range(4):
            rows = lists[d]
            for k in range(2):
                meta = rows[4 * s + 2 + k : 4 * s + 3 + k]
                alive = (meta >= 65536).astype(I32)
                both = rows[4 * s + 1 : 4 * s + 2]
                negative = (both & 65535) if k == 0 else (both >> 16)
                edge = rows[4 * s : 4 * s + 1, k * PAD : (k + 1) * PAD]
                for j in range(2):
                    mine = alive * (before == 2 * core + j).astype(I32)
                    edge_words[j] += edge * mine[:, :PAD]
                    negative_words[j] += negative * mine
                    meta_words[j] += meta * mine
                before = before + alive
        lane1 = lax.broadcasted_iota(I32, (1, 1024), 1)
        for j in range(2):
            valid = lane1[:, :PAD] < (meta_words[j][:, :PAD] >> 16)
            at = 2 * s + j
            sel[at, 0:1, 0:PAD] = jnp.where(valid, edge_words[j] & 65535, -1)
            sel[at, 1:2, 0:PAD] = jnp.where(valid, edge_words[j] >> 16, -1)
            sel[at, 2:3, :] = jnp.where(lane1 < negs, negative_words[j], -1)
            sel[at, 3:4, :] = meta_words[j] & 1
            sel[at, 4:5, 0:PAD] = valid.astype(I32)

    slab_copies[1].wait_send()
    slab_copies[0] = send_slab(0)

    def operator(table, at):
        second = sel[at, 3:4, 0:width].astype(F32)
        return (
            table[0].astype(F32) * (1.0 - second) + table[1].astype(F32) * second
        ).astype(BF16)

    def queries(s):
        for j in range(2):
            at = 2 * s + j
            ohs[at] = onehot(4 * quarter, 0, sel[at, 0:1, 0:PAD])
            vectors = dot(emb[...], ohs[at]).astype(BF16)
            svt[at] = vectors
            qt[at] = dot(operator(opt, at), vectors).astype(BF16)
            times = dot(onehot(2 * quarter, 2 * xh * quarter, sel[at, 2:3, :]), jnp.ones((1024, 128), BF16))
            cnt[at] = times * (0.5 * negs**-0.5)

    def forward(s):
        slab_copies[s].wait_recv()
        return send(
            slabt.at[s, core], slabt.at[s, core], fwd_s.at[s], fwd_r.at[s], sibling
        )

    def halve(s):
        turn = eye(quarter) * jnp.asarray(0.5, BF16)
        for h in range(2):
            slab[h * quarter : (h + 1) * quarter] = dot_nt(turn, slabt[s, h]).astype(BF16)

    def score(s, js):
        turned = jnp.concatenate([slabt[s, 0], slabt[s, 1]], axis=1)
        mains, seconds = [], []
        for j in js:
            at = 2 * s + j
            oht[at] = onehot(2 * quarter, 2 * xh * quarter, sel[at, 1:2, 0:PAD])
            query = qt[at]
            target = dot(turned, oht[at])
            positive = jnp.sum(query.astype(F32) * target, axis=0, keepdims=True)
            positive_grad = -sel[at, 4:5, 0:PAD].astype(F32) * jax.nn.sigmoid(-positive)
            pgs[at, 0:1] = positive_grad
            bent = jnp.tanh(dot(slab[...], query))
            times = jnp.concatenate([cnt[at]] * (PAD // 128), axis=1)
            ngm[at] = (times * bent + times).astype(BF16)
            grad = positive_grad * target + dot(turned, ngm[at])
            high = grad.astype(BF16)
            qhl[at, :, 0:PAD] = high
            qhl[at, :, PAD:] = (grad - high.astype(F32)).astype(BF16)
            mains.append(dot_nt(svt[at], high))
            seconds.append(sel[at, 3:4, 0:128].astype(F32))
        return mains, seconds

    n = width // 16

    def accumulate(s, k, mains, seconds):
        first = jnp.where(k == 0, 1.0, 0.0)
        shares = [first + second * (1.0 - 2.0 * first) for second in seconds]
        for t in range(3):
            tiles = sum(
                main[:, 128 * t : 128 * t + 128] * share for main, share in zip(mains, shares)
            ).reshape(n, 16, 128)
            acc[k, n * t : n * t + n] = tiles if s == 1 else acc[k, n * t : n * t + n] + tiles
        last = sum(
            main[:, 384:width] * share[:, : width - 384] for main, share in zip(mains, shares)
        )
        last = jnp.concatenate([last, jnp.zeros((width, PAD - width), F32)], axis=1)
        if s == 1:
            acc_last[k] = last
            return
        last = acc_last[k] + last
        last = jnp.concatenate([last, jnp.zeros((PAD - width, 128), F32)], axis=0).T
        for t in range(4):
            acc[k, 3 * n + t] = last[:16, 128 * t : 128 * t + 128]
        acc[k, 3 * n + 4] = jnp.zeros((16, 128), F32)

    queries(1)
    forwards = [forward(1)]
    queries(0)
    forwards[0].wait_recv()
    halve(1)
    one = score(1, (0,))
    forwards.append(forward(0))
    two = score(1, (1,))
    for k in range(2):
        accumulate(1, k, one[0] + two[0], one[1] + two[1])
    forwards[1].wait_recv()
    halve(0)
    found = score(0, (0, 1))
    accumulate(0, 1 - core, *found)
    acc_out[...] = acc[1 - core].astype(BF16)
    copy0 = send(acc_out, acc_in, ar0_s, ar0_r, sibling)
    accumulate(0, core, *found)
    copy0.wait_recv()
    red[...] = acc[core] + acc_in[...].astype(F32)
    red_out[...] = red[...].astype(BF16)
    copies1 = []
    for k in (2, 1, 3):
        copies1.append(
            send(red_out.at[pl.ds(10 * x_at(k), 10)], r1.at[0, k - 1], ar1_s.at[0, k - 1], ar1_r.at[0, k - 1], along_x(k))
        )
        copies1.append(
            send(red_out.at[pl.ds(40 + 10 * y_at(k), 10)], r1.at[1, k - 1], ar1_s.at[1, k - 1], ar1_r.at[1, k - 1], along_y(k))
        )

    for s in range(2):
        positives = [(pgs[at, 0:1] * qt[at].astype(F32)).astype(BF16) for at in (2 * s, 2 * s + 1)]
        left = jnp.concatenate([qt[2 * s], qt[2 * s + 1]] + positives, axis=1)
        for h in range(2):
            rows = slice(h * quarter, (h + 1) * quarter)
            parts = [ngm[2 * s, rows], ngm[2 * s + 1, rows], oht[2 * s, rows], oht[2 * s + 1, rows]]
            tsum[s, h] = dot_nt(left, jnp.concatenate(parts, axis=1))
    tx_copies = [
        send(tsum.at[s, 1 - core], tsum_in.at[s], tx_s.at[s], tx_r.at[s], sibling)
        for s in range(2)
    ]

    for at in range(4):
        turned = operator(rel, at)
        both = jnp.concatenate([qhl[at, :, 0:PAD], qhl[at, :, PAD:]], axis=0)
        sgt[at] = dot(jnp.concatenate([turned, turned], axis=1), both).astype(BF16)

    for copy in copies1:
        copy.wait_recv()
    for h, at in ((0, 10 * x), (1, 40 + 10 * y)):
        total = red[pl.ds(at, 10)]
        for k in range(3):
            total += r1[h, k].astype(F32)
        s1[h, 0:10] = total
    r2[0, y] = s1[0, pl.ds(3 * y, 3)]
    r2[1, x] = s1[1, pl.ds(3 * x, 3)]
    copies2 = []
    for k in (2, 1, 3):
        copies2.append(
            send(s1.at[0, pl.ds(3 * y_at(k), 3)], r2.at[0, y], ar2_s.at[0, k - 1], ar2_r.at[0, k - 1], along_y(k))
        )
        copies2.append(
            send(s1.at[1, pl.ds(3 * x_at(k), 3)], r2.at[1, x], ar2_s.at[1, k - 1], ar2_r.at[1, k - 1], along_x(k))
        )

    for copy in tx_copies:
        copy.wait_recv()
    ret[0] = (tsum[0, core] + tsum_in[0]).astype(BF16)
    ret_copies = [send(ret.at[0], ret_in.at[0], ret_s.at[0], ret_r.at[0], partner)]

    left = jnp.concatenate([sgt[at] for at in range(4)], axis=1)
    for q in range(4):
        rows = slice(q * quarter, (q + 1) * quarter)
        ssum[q // 2, q % 2] = dot_nt(left, jnp.concatenate([ohs[at, rows] for at in range(4)], axis=1))
    sx_copies = [
        send(ssum.at[h, 1 - core], ssum_in.at[h], sx_s.at[h], sx_r.at[h], sibling)
        for h in range(2)
    ]

    for copy in copies2:
        copy.wait_recv()
    for h in range(2):
        total = (r2[h, 0] + r2[h, 1]) + (r2[h, 2] + r2[h, 3])
        zx[z, 3 * h : 3 * h + 3] = total.astype(BF16)
    copies3 = [
        send(zx.at[z], zx.at[z], ar3_s.at[k - 1], ar3_r.at[k - 1], along_z(k))
        for k in sorted(range(1, n_z), key=lambda k: -min(k, n_z - k))
    ]

    for copy in sx_copies:
        copy.wait_recv()
    half[...] = (ssum[1 - xh, core] + ssum_in[1 - xh]).astype(BF16)
    sy_copy = send(half, half_in, sy_s, sy_r, mate)
    ret_copies[0].wait_recv()
    passed = ret_in[0].astype(F32) * jnp.where(xl == 1, 1.0, 0.0)
    ret[1] = (tsum[1, core] + tsum_in[1] + passed).astype(BF16)
    ret_copies.append(send(ret.at[1], ret_in.at[1], ret_s.at[1], ret_r.at[1], along_blk(-2)))
    for copy in copies3:
        copy.wait_recv()
    total = zx[0].astype(F32)
    for k in range(1, n_z):
        total += zx[k].astype(F32)
    total = total.astype(BF16)
    g2[0, y] = total[0:3]
    g2[1, x] = total[3:6]
    copies = []
    for k in (2, 1, 3):
        copies.append(send(g2.at[0, y], g2.at[0, y], ag2_s.at[0, k - 1], ag2_r.at[0, k - 1], along_y(k)))
        copies.append(send(g2.at[1, x], g2.at[1, x], ag2_s.at[1, k - 1], ag2_r.at[1, k - 1], along_x(k)))
    sends = list(copies)
    for copy in copies:
        copy.wait_recv()
    for h, at in ((0, x), (1, y)):
        for k in range(3):
            g1[h, at, 3 * k : 3 * k + 3] = g2[h, k]
        g1[h, at, 9] = g2[h, 3, 0]
    copies = []
    for k in (2, 1, 3):
        copies.append(send(g1.at[0, x], g1.at[0, x], ag1_s.at[0, k - 1], ag1_r.at[0, k - 1], along_x(k)))
        copies.append(send(g1.at[1, y], g1.at[1, y], ag1_s.at[1, k - 1], ag1_r.at[1, k - 1], along_y(k)))
    sends += copies
    handed = [
        send(g1.at[h, at], g_other.at[h, at], ag0_s.at[h, 0], ag0_r.at[h, 0], sibling)
        for h, at in ((0, x), (1, y))
    ]

    for i, k in ((1, 1), (2, 3), (0, 2)):
        copies[2 * i].wait_recv()
        copies[2 * i + 1].wait_recv()
        for h, at in ((0, x_at(4 - k)), (1, y_at(4 - k))):
            handed.append(
                send(g1.at[h, at], g_other.at[h, at], ag0_s.at[h, k], ag0_r.at[h, k], sibling)
            )

    def write(k, tiles):
        for t in range(3):
            rel_out[k, :, 128 * t : 128 * t + 128] = tiles[n * t : n * t + n].reshape(width, 128)
        rest = jnp.concatenate([tiles[3 * n + t].astype(F32) for t in range(4)], axis=1)
        rest = jnp.concatenate([rest, jnp.zeros((112, PAD), F32)], axis=0)
        rel_out[k, :, 384:width] = rest.T[:width, : width - 384].astype(BF16)

    sy_copy.wait_recv()
    ret_copies[1].wait_recv()
    total = (ssum[xh, core] + ssum_in[xh]) + half_in[...].astype(F32)
    mine = ret_in[0].astype(F32) * jnp.where(xl == 0, 1.0, 0.0)
    total = total + (mine + ret_in[1].astype(F32))
    ent_out[...] = total

    write(core, g1[...].reshape(TILES, 16, 128))
    for copy in handed:
        copy.wait_recv()
    write(1 - core, g_other[...].reshape(TILES, 16, 128))

    for copy in [slab_copies[0]] + forwards + [copy0, sy_copy] + handed + sends:
        copy.wait_send()
    for copy in tx_copies + copies1 + copies2 + copies3 + sx_copies + ret_copies:
        copy.wait_send()


def hand_over(entity, relation, entity_out, relation_out):
    entity_out[...] = entity[...]
    relation_out[...] = relation[...].astype(F32)


def on_device(n_y, n_z, embeddings, relations, *lists):
    rows, width = embeddings.shape
    quarter = rows // 4
    span = lists[0].shape[1] // 2
    negs = lists[2].shape[2]
    dma = pltpu.SemaphoreType.DMA
    vmem, smem = pl.BlockSpec(memory_space=pltpu.VMEM), pl.BlockSpec(memory_space=pltpu.SMEM)

    def buffer(*shape, kind=F32):
        return pltpu.VMEM(shape, kind)

    scratch = [
        buffer(*embeddings.shape[::-1], kind=BF16),
        buffer(2, width, width, kind=BF16),
        buffer(2, width, width, kind=BF16),
        buffer(2, 8, 1024, kind=I32),
        buffer(4, 8, 1024, kind=I32),
        buffer(4, 8, 1024, kind=I32),
        buffer(4, rows, PAD, kind=BF16),
        buffer(4, width, PAD, kind=BF16),
        buffer(4, width, PAD, kind=BF16),
        buffer(4, rows // 2, 128),
        buffer(2, 2, width, quarter, kind=BF16),
        buffer(rows // 2, width, kind=BF16),
        buffer(4, rows // 2, PAD, kind=BF16),
        buffer(4, rows // 2, PAD, kind=BF16),
        buffer(4, 8, PAD),
        buffer(4, width, 2 * PAD, kind=BF16),
        buffer(4, width, PAD, kind=BF16),
        buffer(2, TILES, 16, 128),
        buffer(2, width, 128),
        buffer(TILES, 16, 128, kind=BF16),
        buffer(TILES, 16, 128, kind=BF16),
        buffer(TILES, 16, 128),
        buffer(TILES, 16, 128, kind=BF16),
        buffer(2, 3, 10, 16, 128, kind=BF16),
        buffer(2, 12, 16, 128),
        buffer(2, 4, 3, 16, 128),
        buffer(n_z, 6, 16, 128, kind=BF16),
        buffer(2, 4, 3, 16, 128, kind=BF16),
        buffer(2, 4, 10, 16, 128, kind=BF16),
        buffer(2, 4, 10, 16, 128, kind=BF16),
        buffer(2, 2, width, quarter),
        buffer(2, width, quarter),
        buffer(2, width, quarter, kind=BF16),
        buffer(2, width, quarter, kind=BF16),
        buffer(2, 2, width, quarter),
        buffer(2, width, quarter),
        buffer(width, quarter, kind=BF16),
        buffer(width, quarter, kind=BF16),
        dma((2,)),
    ]
    for shape in (
        (3,), (2,), (2,), None, (2, 3), (2, 3), (n_z - 1,),
        (2, 3), (2, 3), (2, 4), (2,), (2,), (2,), None,
    ):
        scratch += [dma if shape is None else dma(shape)] * 2
    entity, relation = pl.pallas_call(
        functools.partial(kernel, n_y, n_z, span, negs),
        out_shape=(
            jax.ShapeDtypeStruct((width, quarter), F32),
            jax.ShapeDtypeStruct(relations.shape, BF16),
        ),
        in_specs=[pl.BlockSpec(memory_space=pl.ANY)] * 2 + [vmem] * 3 + [smem] * 2,
        out_specs=(vmem, vmem),
        scratch_shapes=scratch,
        compiler_params=pltpu.CompilerParams(
            collective_id=0, has_side_effects=True, vmem_limit_bytes=56 * 2**20
        ),
    )(embeddings.T, relations, *lists[:-1], lists[-1].T)
    blocks = [
        pl.BlockSpec((width // 2, quarter), lambda i: (i, 0)),
        pl.BlockSpec((1, width, width), lambda i: (i, 0, 0)),
    ]
    entity, relation = pl.pallas_call(
        hand_over,
        out_shape=(
            jax.ShapeDtypeStruct(entity.shape, F32),
            jax.ShapeDtypeStruct(relation.shape, F32),
        ),
        grid=(2,),
        in_specs=blocks,
        out_specs=tuple(blocks),
    )(entity, relation)
    return entity.T, relation


def solution(mesh):
    n_y = 4
    n_z = mesh.shape["blk"] // (2 * n_y)
    return jax.shard_map(
        functools.partial(on_device, n_y, n_z),
        mesh=mesh,
        in_specs=(
            P("blk", None),
            P(),
            P(None, ("blk", "rep")),
            P(None, ("blk", "rep")),
            P(None, ("blk", "rep"), None),
            P(None, ("blk", "rep")),
            P(None, ("blk", "rep")),
        ),
        out_specs=(P(("blk", "rep"), None), P()),
        check_vma=False,
    )
```

```python
import functools

import jax
import jax.numpy as jnp
from jax import lax
from jax.experimental import pallas as pl
from jax.experimental.pallas import tpu as pltpu
from jax.sharding import PartitionSpec as P

MESH = pl.DeviceIdType.MESH
F32, BF16, I32 = jnp.float32, jnp.bfloat16, jnp.int32
PAD = 512
TILES = 80


def dot(a, b):
    return lax.dot_general(a, b, (((1,), (0,)), ((), ())), preferred_element_type=F32)


def dot_nt(a, b):
    return lax.dot_general(a, b, (((1,), (1,)), ((), ())), preferred_element_type=F32)


def eye(n):
    return (
        lax.broadcasted_iota(I32, (n, n), 0) == lax.broadcasted_iota(I32, (n, n), 1)
    ).astype(F32).astype(BF16)


def onehot(rows, base, index):
    shape = (rows, index.shape[1])
    return (lax.broadcasted_iota(I32, shape, 0) + base == index).astype(F32).astype(BF16)


def kernel(
    n_y, n_z, span, negs,
    emb_hbm, rel_hbm, src, tgt, neg, srel, ecnt,
    ent_out, rel_out,
    emb, rel, opt, raw, lists, sel, ohs, svt, qt, cnt, slabt, slab, oht, ngm, pgs, qhl, sgt,
    acc, acc_last, acc_out, acc_in, red, red_out, r1, s1, r2, zx, g2, g1, g_other,
    tsum, tsum_in, ret, ret_in, ssum, ssum_in, half, half_in,
    load, idx_s, idx_r, slab_s, slab_r, fwd_s, fwd_r, ar0_s, ar0_r, ar1_s, ar1_r, ar2_s, ar2_r, ar3_s, ar3_r,
    ag2_s, ag2_r, ag1_s, ag1_r, ag0_s, ag0_r, tx_s, tx_r, ret_s, ret_r, sx_s, sx_r, sy_s, sy_r,
):
    width = emb.shape[0]
    n_blk = 2 * n_y * n_z
    quarter = emb.shape[1] // 4
    b, r = lax.axis_index("blk"), lax.axis_index("rep")
    xh, core = r // 2, lax.rem(r, 2)
    xl, y, z = lax.rem(b, 2), lax.rem(b // 2, n_y), b // (2 * n_y)
    x = xh * 2 + xl
    sibling = (b, xh * 2 + 1 - core)
    mate = (b, (1 - xh) * 2 + core)
    partner = (b + 1 - 2 * xl, r)

    def along_blk(k):
        return (lax.rem(b + k + n_blk, n_blk), r)

    def along_rep(k):
        return (b, lax.rem(r + k, 4))

    def x_at(k):
        return lax.rem(x + k, 4)

    def y_at(k):
        return lax.rem(y + k, n_y)

    def z_at(k):
        return lax.rem(z + k, n_z)

    def along_x(k):
        there = x_at(k)
        return ((z * n_y + y) * 2 + lax.rem(there, 2), (there // 2) * 2 + core)

    def along_y(k):
        return ((z * n_y + y_at(k)) * 2 + xl, r)

    def along_z(k):
        return ((z_at(k) * n_y + y) * 2 + xl, r)

    def send(source, target, sent, received, device):
        copy = pltpu.make_async_remote_copy(
            src_ref=source, dst_ref=target, send_sem=sent, recv_sem=received,
            device_id=device, device_id_type=MESH,
        )
        copy.start()
        return copy

    barrier = pltpu.get_barrier_semaphore()
    peers = [along_blk(k) for k in (1, 2, -1, -2)] + [along_rep(k) for k in (1, 2, 3)]
    peers += [along_x(k) for k in (1, 2, 3)] + [along_y(k) for k in range(1, n_y)]
    peers += [along_z(k) for k in range(1, n_z)]
    for peer in peers:
        pl.semaphore_signal(barrier, inc=1, device_id=peer, device_id_type=MESH)

    loads = [
        pltpu.make_async_copy(emb_hbm, emb, load.at[0]),
        pltpu.make_async_copy(rel_hbm, rel, load.at[1]),
    ]
    for copy in loads:
        copy.start()
    lane = lax.broadcasted_iota(I32, (8, 1024), 1)
    row = lax.broadcasted_iota(I32, (8, 1024), 0)
    raw[...] = jnp.zeros(raw.shape, I32)
    raw[0, 0:2, 0 : 2 * span] = src[...]
    raw[0, 2:4, 0 : 2 * span] = tgt[...]
    for s in range(2):
        raw[1, 2 * s : 2 * s + 2, 0:negs] = neg[s]
    edges = raw[0]
    second = pltpu.roll(edges, PAD - span, 1)
    edges = jnp.where(lane < PAD, edges, second)
    negatives = raw[1]
    packed = jnp.zeros((8, 1024), I32)
    for s in range(2):
        words = edges[s : s + 1] + edges[2 + s : 3 + s] * 65536
        packed = jnp.where(row == 4 * s, words, packed)
        words = negatives[2 * s : 2 * s + 1] + negatives[2 * s + 1 : 2 * s + 2] * 65536
        packed = jnp.where(row == 4 * s + 1, words, packed)
        for k in range(2):
            live = jnp.clip(ecnt[0, s] - k * span, 0, span)
            packed = jnp.where(row == 4 * s + 2 + k, srel[s, k] + live * 65536, packed)
    lists[r] = packed

    pl.semaphore_wait(barrier, len(peers))

    index_copies = [
        send(lists.at[r], lists.at[r], idx_s.at[k - 1], idx_r.at[k - 1], along_rep(k))
        for k in (2, 1, 3)
    ]
    here = pl.ds(pl.multiple_of(r * quarter, quarter), quarter)

    def send_slab(s):
        return send(
            emb_hbm.at[:, here], slabt.at[s, core], slab_s.at[s], slab_r.at[s], along_blk(s + 1)
        )

    slab_copies = {1: send_slab(1)}

    for copy in loads:
        copy.wait()
    unit = eye(width)
    for k in range(2):
        opt[k] = dot_nt(unit, rel[k]).astype(BF16)
    s1[...] = jnp.zeros(s1.shape, F32)
    for copy in index_copies:
        copy.wait()

    for s in range(2):
        before = jnp.zeros((1, 1024), I32)
        edge_words = [jnp.zeros((1, PAD), I32) for j in range(2)]
        negative_words = [jnp.zeros((1, 1024), I32) for j in range(2)]
        meta_words = [jnp.zeros((1, 1024), I32) for j in range(2)]
        for d in range(4):
            rows = lists[d]
            for k in range(2):
                meta = rows[4 * s + 2 + k : 4 * s + 3 + k]
                alive = (meta >= 65536).astype(I32)
                both = rows[4 * s + 1 : 4 * s + 2]
                negative = (both & 65535) if k == 0 else (both >> 16)
                edge = rows[4 * s : 4 * s + 1, k * PAD : (k + 1) * PAD]
                for j in range(2):
                    mine = alive * (before == 2 * core + j).astype(I32)
                    edge_words[j] += edge * mine[:, :PAD]
                    negative_words[j] += negative * mine
                    meta_words[j] += meta * mine
                before = before + alive
        lane1 = lax.broadcasted_iota(I32, (1, 1024), 1)
        for j in range(2):
            valid = lane1[:, :PAD] < (meta_words[j][:, :PAD] >> 16)
            at = 2 * s + j
            sel[at, 0:1, 0:PAD] = jnp.where(valid, edge_words[j] & 65535, -1)
            sel[at, 1:2, 0:PAD] = jnp.where(valid, edge_words[j] >> 16, -1)
            sel[at, 2:3, :] = jnp.where(lane1 < negs, negative_words[j], -1)
            sel[at, 3:4, :] = meta_words[j] & 1
            sel[at, 4:5, 0:PAD] = valid.astype(I32)

    slab_copies[1].wait_send()
    slab_copies[0] = send_slab(0)

    def operator(table, at):
        second = sel[at, 3:4, 0:width].astype(F32)
        return (
            table[0].astype(F32) * (1.0 - second) + table[1].astype(F32) * second
        ).astype(BF16)

    def queries(s):
        for j in range(2):
            at = 2 * s + j
            ohs[at] = onehot(4 * quarter, 0, sel[at, 0:1, 0:PAD])
            oht[at] = onehot(2 * quarter, 2 * xh * quarter, sel[at, 1:2, 0:PAD])
            vectors = dot(emb[...], ohs[at]).astype(BF16)
            svt[at] = vectors
            qt[at] = dot(operator(opt, at), vectors).astype(BF16)
            times = dot(onehot(2 * quarter, 2 * xh * quarter, sel[at, 2:3, :]), jnp.ones((1024, 128), BF16))
            cnt[at] = times * (0.5 * negs**-0.5)

    def forward(s):
        slab_copies[s].wait_recv()
        return send(
            slabt.at[s, core], slabt.at[s, core], fwd_s.at[s], fwd_r.at[s], sibling
        )

    def halve(s):
        turn = eye(quarter) * jnp.asarray(0.5, BF16)
        for h in range(2):
            slab[h * quarter : (h + 1) * quarter] = dot_nt(turn, slabt[s, h]).astype(BF16)

    def score(s, js):
        turned = jnp.concatenate([slabt[s, 0], slabt[s, 1]], axis=1)
        mains, seconds = [], []
        for j in js:
            at = 2 * s + j
            query = qt[at]
            target = dot(turned, oht[at])
            positive = jnp.sum(query.astype(F32) * target, axis=0, keepdims=True)
            positive_grad = -sel[at, 4:5, 0:PAD].astype(F32) * jax.nn.sigmoid(-positive)
            pgs[at, 0:1] = positive_grad
            bent = jnp.tanh(dot(slab[...], query))
            times = jnp.concatenate([cnt[at]] * (PAD // 128), axis=1)
            ngm[at] = (times * bent + times).astype(BF16)
            grad = positive_grad * target + dot(turned, ngm[at])
            high = grad.astype(BF16)
            qhl[at, :, 0:PAD] = high
            qhl[at, :, PAD:] = (grad - high.astype(F32)).astype(BF16)
            mains.append(dot_nt(svt[at], high))
            seconds.append(sel[at, 3:4, 0:128].astype(F32))
        return mains, seconds

    n = width // 16

    def accumulate(s, k, mains, seconds):
        first = jnp.where(k == 0, 1.0, 0.0)
        shares = [first + second * (1.0 - 2.0 * first) for second in seconds]
        for t in range(3):
            tiles = sum(
                main[:, 128 * t : 128 * t + 128] * share for main, share in zip(mains, shares)
            ).reshape(n, 16, 128)
            acc[k, n * t : n * t + n] = tiles if s == 1 else acc[k, n * t : n * t + n] + tiles
        last = sum(
            main[:, 384:width] * share[:, : width - 384] for main, share in zip(mains, shares)
        )
        last = jnp.concatenate([last, jnp.zeros((width, PAD - width), F32)], axis=1)
        if s == 1:
            acc_last[k] = last
            return
        last = acc_last[k] + last
        last = jnp.concatenate([last, jnp.zeros((PAD - width, 128), F32)], axis=0).T
        for t in range(4):
            acc[k, 3 * n + t] = last[:16, 128 * t : 128 * t + 128]
        acc[k, 3 * n + 4] = jnp.zeros((16, 128), F32)

    queries(1)
    forwards = [forward(1)]
    queries(0)
    forwards[0].wait_recv()
    halve(1)
    one = score(1, (0,))
    forwards.append(forward(0))
    two = score(1, (1,))
    for k in range(2):
        accumulate(1, k, one[0] + two[0], one[1] + two[1])
    forwards[1].wait_recv()
    halve(0)
    found = score(0, (0, 1))
    accumulate(0, 1 - core, *found)
    acc_out[...] = acc[1 - core].astype(BF16)
    copy0 = send(acc_out, acc_in, ar0_s, ar0_r, sibling)
    accumulate(0, core, *found)
    copy0.wait_recv()
    red[...] = acc[core] + acc_in[...].astype(F32)
    red_out[...] = red[...].astype(BF16)
    copies1 = []
    for k in (2, 1, 3):
        copies1.append(
            send(red_out.at[pl.ds(10 * x_at(k), 10)], r1.at[0, k - 1], ar1_s.at[0, k - 1], ar1_r.at[0, k - 1], along_x(k))
        )
        copies1.append(
            send(red_out.at[pl.ds(40 + 10 * y_at(k), 10)], r1.at[1, k - 1], ar1_s.at[1, k - 1], ar1_r.at[1, k - 1], along_y(k))
        )

    for s in range(2):
        positives = [(pgs[at, 0:1] * qt[at].astype(F32)).astype(BF16) for at in (2 * s, 2 * s + 1)]
        left = jnp.concatenate([qt[2 * s], qt[2 * s + 1]] + positives, axis=1)
        for h in range(2):
            rows = slice(h * quarter, (h + 1) * quarter)
            parts = [ngm[2 * s, rows], ngm[2 * s + 1, rows], oht[2 * s, rows], oht[2 * s + 1, rows]]
            tsum[s, h] = dot_nt(left, jnp.concatenate(parts, axis=1))
    tx_copies = [
        send(tsum.at[s, 1 - core], tsum_in.at[s], tx_s.at[s], tx_r.at[s], sibling)
        for s in range(2)
    ]

    for at in range(4):
        turned = operator(rel, at)
        both = jnp.concatenate([qhl[at, :, 0:PAD], qhl[at, :, PAD:]], axis=0)
        sgt[at] = dot(jnp.concatenate([turned, turned], axis=1), both).astype(BF16)

    for copy in copies1:
        copy.wait_recv()
    for h, at in ((0, 10 * x), (1, 40 + 10 * y)):
        total = red[pl.ds(at, 10)]
        for k in range(3):
            total += r1[h, k].astype(F32)
        s1[h, 0:10] = total
    r2[0, y] = s1[0, pl.ds(3 * y, 3)]
    r2[1, x] = s1[1, pl.ds(3 * x, 3)]
    copies2 = []
    for k in (2, 1, 3):
        copies2.append(
            send(s1.at[0, pl.ds(3 * y_at(k), 3)], r2.at[0, y], ar2_s.at[0, k - 1], ar2_r.at[0, k - 1], along_y(k))
        )
        copies2.append(
            send(s1.at[1, pl.ds(3 * x_at(k), 3)], r2.at[1, x], ar2_s.at[1, k - 1], ar2_r.at[1, k - 1], along_x(k))
        )

    for copy in tx_copies:
        copy.wait_recv()
    ret[0] = (tsum[0, core] + tsum_in[0]).astype(BF16)
    ret_copies = [send(ret.at[0], ret_in.at[0], ret_s.at[0], ret_r.at[0], partner)]

    left = jnp.concatenate([sgt[at] for at in range(4)], axis=1)
    for q in range(4):
        rows = slice(q * quarter, (q + 1) * quarter)
        ssum[q // 2, q % 2] = dot_nt(left, jnp.concatenate([ohs[at, rows] for at in range(4)], axis=1))
    sx_copies = [
        send(ssum.at[h, 1 - core], ssum_in.at[h], sx_s.at[h], sx_r.at[h], sibling)
        for h in range(2)
    ]

    for copy in copies2:
        copy.wait_recv()
    for h in range(2):
        total = (r2[h, 0] + r2[h, 1]) + (r2[h, 2] + r2[h, 3])
        zx[z, 3 * h : 3 * h + 3] = total.astype(BF16)
    copies3 = [
        send(zx.at[z], zx.at[z], ar3_s.at[k - 1], ar3_r.at[k - 1], along_z(k))
        for k in sorted(range(1, n_z), key=lambda k: -min(k, n_z - k))
    ]

    for copy in sx_copies:
        copy.wait_recv()
    half[...] = (ssum[1 - xh, core] + ssum_in[1 - xh]).astype(BF16)
    sy_copy = send(half, half_in, sy_s, sy_r, mate)
    ret_copies[0].wait_recv()
    passed = ret_in[0].astype(F32) * jnp.where(xl == 1, 1.0, 0.0)
    ret[1] = (tsum[1, core] + tsum_in[1] + passed).astype(BF16)
    ret_copies.append(send(ret.at[1], ret_in.at[1], ret_s.at[1], ret_r.at[1], along_blk(-2)))
    for copy in copies3:
        copy.wait_recv()
    total = zx[0].astype(F32)
    for k in range(1, n_z):
        total += zx[k].astype(F32)
    total = total.astype(BF16)
    g2[0, y] = total[0:3]
    g2[1, x] = total[3:6]
    copies = []
    for k in (2, 1, 3):
        copies.append(send(g2.at[0, y], g2.at[0, y], ag2_s.at[0, k - 1], ag2_r.at[0, k - 1], along_y(k)))
        copies.append(send(g2.at[1, x], g2.at[1, x], ag2_s.at[1, k - 1], ag2_r.at[1, k - 1], along_x(k)))
    sends = list(copies)
    for copy in copies:
        copy.wait_recv()
    for h, at in ((0, x), (1, y)):
        for k in range(3):
            g1[h, at, 3 * k : 3 * k + 3] = g2[h, k]
        g1[h, at, 9] = g2[h, 3, 0]
    copies = []
    for k in (2, 1, 3):
        copies.append(send(g1.at[0, x], g1.at[0, x], ag1_s.at[0, k - 1], ag1_r.at[0, k - 1], along_x(k)))
        copies.append(send(g1.at[1, y], g1.at[1, y], ag1_s.at[1, k - 1], ag1_r.at[1, k - 1], along_y(k)))
    sends += copies
    handed = [
        send(g1.at[h, at], g_other.at[h, at], ag0_s.at[h, 0], ag0_r.at[h, 0], sibling)
        for h, at in ((0, x), (1, y))
    ]

    for i, k in ((1, 1), (2, 3), (0, 2)):
        copies[2 * i].wait_recv()
        copies[2 * i + 1].wait_recv()
        for h, at in ((0, x_at(4 - k)), (1, y_at(4 - k))):
            handed.append(
                send(g1.at[h, at], g_other.at[h, at], ag0_s.at[h, k], ag0_r.at[h, k], sibling)
            )

    def write(k, tiles):
        for t in range(3):
            rel_out[k, :, 128 * t : 128 * t + 128] = tiles[n * t : n * t + n].reshape(width, 128)
        rest = jnp.concatenate([tiles[3 * n + t].astype(F32) for t in range(4)], axis=1)
        rest = jnp.concatenate([rest, jnp.zeros((112, PAD), F32)], axis=0)
        rel_out[k, :, 384:width] = rest.T[:width, : width - 384].astype(BF16)

    sy_copy.wait_recv()
    ret_copies[1].wait_recv()
    total = (ssum[xh, core] + ssum_in[xh]) + half_in[...].astype(F32)
    mine = ret_in[0].astype(F32) * jnp.where(xl == 0, 1.0, 0.0)
    total = total + (mine + ret_in[1].astype(F32))
    ent_out[...] = total

    write(core, g1[...].reshape(TILES, 16, 128))
    for copy in handed:
        copy.wait_recv()
    write(1 - core, g_other[...].reshape(TILES, 16, 128))

    for copy in [slab_copies[0]] + forwards + [copy0, sy_copy] + handed + sends:
        copy.wait_send()
    for copy in tx_copies + copies1 + copies2 + copies3 + sx_copies + ret_copies:
        copy.wait_send()


def hand_over(entity, relation, entity_out, relation_out):
    entity_out[...] = entity[...]
    relation_out[...] = relation[...].astype(F32)


def on_device(n_y, n_z, embeddings, relations, *lists):
    rows, width = embeddings.shape
    quarter = rows // 4
    span = lists[0].shape[1] // 2
    negs = lists[2].shape[2]
    dma = pltpu.SemaphoreType.DMA
    vmem, smem = pl.BlockSpec(memory_space=pltpu.VMEM), pl.BlockSpec(memory_space=pltpu.SMEM)

    def buffer(*shape, kind=F32):
        return pltpu.VMEM(shape, kind)

    scratch = [
        buffer(*embeddings.shape[::-1], kind=BF16),
        buffer(2, width, width, kind=BF16),
        buffer(2, width, width, kind=BF16),
        buffer(2, 8, 1024, kind=I32),
        buffer(4, 8, 1024, kind=I32),
        buffer(4, 8, 1024, kind=I32),
        buffer(4, rows, PAD, kind=BF16),
        buffer(4, width, PAD, kind=BF16),
        buffer(4, width, PAD, kind=BF16),
        buffer(4, rows // 2, 128),
        buffer(2, 2, width, quarter, kind=BF16),
        buffer(rows // 2, width, kind=BF16),
        buffer(4, rows // 2, PAD, kind=BF16),
        buffer(4, rows // 2, PAD, kind=BF16),
        buffer(4, 8, PAD),
        buffer(4, width, 2 * PAD, kind=BF16),
        buffer(4, width, PAD, kind=BF16),
        buffer(2, TILES, 16, 128),
        buffer(2, width, 128),
        buffer(TILES, 16, 128, kind=BF16),
        buffer(TILES, 16, 128, kind=BF16),
        buffer(TILES, 16, 128),
        buffer(TILES, 16, 128, kind=BF16),
        buffer(2, 3, 10, 16, 128, kind=BF16),
        buffer(2, 12, 16, 128),
        buffer(2, 4, 3, 16, 128),
        buffer(n_z, 6, 16, 128, kind=BF16),
        buffer(2, 4, 3, 16, 128, kind=BF16),
        buffer(2, 4, 10, 16, 128, kind=BF16),
        buffer(2, 4, 10, 16, 128, kind=BF16),
        buffer(2, 2, width, quarter),
        buffer(2, width, quarter),
        buffer(2, width, quarter, kind=BF16),
        buffer(2, width, quarter, kind=BF16),
        buffer(2, 2, width, quarter),
        buffer(2, width, quarter),
        buffer(width, quarter, kind=BF16),
        buffer(width, quarter, kind=BF16),
        dma((2,)),
    ]
    for shape in (
        (3,), (2,), (2,), None, (2, 3), (2, 3), (n_z - 1,),
        (2, 3), (2, 3), (2, 4), (2,), (2,), (2,), None,
    ):
        scratch += [dma if shape is None else dma(shape)] * 2
    entity, relation = pl.pallas_call(
        functools.partial(kernel, n_y, n_z, span, negs),
        out_shape=(
            jax.ShapeDtypeStruct((width, quarter), F32),
            jax.ShapeDtypeStruct(relations.shape, BF16),
        ),
        in_specs=[pl.BlockSpec(memory_space=pl.ANY)] * 2 + [vmem] * 3 + [smem] * 2,
        out_specs=(vmem, vmem),
        scratch_shapes=scratch,
        compiler_params=pltpu.CompilerParams(
            collective_id=0, has_side_effects=True, vmem_limit_bytes=56 * 2**20
        ),
    )(embeddings.T, relations, *lists[:-1], lists[-1].T)
    blocks = [
        pl.BlockSpec((width // 2, quarter), lambda i: (i, 0)),
        pl.BlockSpec((1, width, width), lambda i: (i, 0, 0)),
    ]
    entity, relation = pl.pallas_call(
        hand_over,
        out_shape=(
            jax.ShapeDtypeStruct(entity.shape, F32),
            jax.ShapeDtypeStruct(relation.shape, F32),
        ),
        grid=(2,),
        in_specs=blocks,
        out_specs=tuple(blocks),
    )(entity, relation)
    return entity.T, relation


def solution(mesh):
    n_y = 4
    n_z = mesh.shape["blk"] // (2 * n_y)
    return jax.shard_map(
        functools.partial(on_device, n_y, n_z),
        mesh=mesh,
        in_specs=(
            P("blk", None),
            P(),
            P(None, ("blk", "rep")),
            P(None, ("blk", "rep")),
            P(None, ("blk", "rep"), None),
            P(None, ("blk", "rep")),
            P(None, ("blk", "rep")),
        ),
        out_specs=(P(("blk", "rep"), None), P()),
        check_vma=False,
    )
```
